256 devices in a mesh: row: 16 (over x, y), col: 8 (over z_lo, core), tp: 2 (over z_hi).
Axes of the slice: x: 4, y: 4, z: 8 (z_hi: 2, z_lo: 4; z = z_hi * 4 + z_lo), core: 2. Of those that a mesh axis runs over, the one named last changes fastest.
Arguments:
- patches: bfloat16 [512, 128, 1536], P(('row', 'col')), may hold values from -6 to 6
- counts: int32 [512], P(('row', 'col')), may hold values from 16 to 128
- text_tokens: bfloat16 [512, 64, 1536], P(('col', 'row')), may hold values from -6 to 6
- partner: int32 [512], replicated, may hold values from 0 to 511, each once
- scale: float32 [1], replicated, may hold values from 4 to 16
- shift: float32 [1], replicated, may hold values from -6 to -2
- img_w_in: bfloat16 [1536, 4096], P('col', 'tp'), may hold values from -0.15625 to 0.15625
- img_w_out: bfloat16 [4096, 1536], P('tp', 'col'), may hold values from -0.09375 to 0.09375
- txt_w_in: bfloat16 [1536, 4096], P('row', 'tp'), may hold values from -0.15625 to 0.15625
- txt_w_out: bfloat16 [4096, 1536], P('tp', 'row'), may hold values from -0.09375 to 0.09375
Outputs:
- grad_patches: bfloat16 [512, 128, 1536], P(('row', 'col'), None, 'tp')
- grad_text: bfloat16 [512, 64, 1536], P(('col', 'row'), None, 'tp')
The draws below stay inside these ranges and needn't reach their ends.
All inputs are finite; a program needn't handle non-finite values.
Results may differ from the reference program's by a relative error of at most 0.0065.
Values may be sent and summed in bfloat16 or wider, within the bound.
A program may use at most 128 MiB of HBM per device.

```python
import math
import jax
import jax.numpy as jnp
from jax import lax

D = 1536
FF = 4096
P_SIZE = 128
L = 64
PAIRS = 512


def place_ends(array, stream_key, low, largest):
    place = [jax.random.randint(jax.random.fold_in(stream_key, axis), (), 0, length) for axis, length in enumerate(array.shape)]
    widest = array.shape.index(max(array.shape))
    neighbour = place[:widest] + [(place[widest] + 1) % array.shape[widest]] + place[widest + 1:]
    return array.at[tuple(place)].set(low).at[tuple(neighbour)].set(largest)


def block_scale(rng, extent, shards, least, top_value):
    factor_of, own = 1.0, jax.random.fold_in(rng, 6)
    for position, shards_of in shards:
        heights = jnp.exp(jax.random.uniform(jax.random.fold_in(own, position), (shards_of,), jnp.float32, least / len(shards), top_value / len(shards)))
        factor_of = factor_of * jnp.repeat(heights, extent[position] // shards_of).reshape([-1 if axis == position else 1 for axis in range(len(extent))])
    return factor_of


def gaussian(rng, dims, scale, reach, split=(), held_as=jnp.bfloat16):
    gain = block_scale(rng, dims, split, -0.22, 0.18) if split else 1.0
    result = jax.random.normal(rng, dims, jnp.float32) * scale * gain
    return jnp.minimum(jnp.maximum(result, -reach), reach).astype(held_as)


def setup_inputs(seed: int = 0) -> dict:
    key_list = jax.random.split(jax.random.key(seed), 11)
    patches = gaussian(key_list[0], (PAIRS, P_SIZE, D), 1.0, 6.0, ((0, 128),))
    counts = place_ends(jax.random.randint(key_list[1], (PAIRS,), P_SIZE // 8, P_SIZE + 1), jax.random.fold_in(key_list[1], 1), P_SIZE // 8, P_SIZE).astype(jnp.int32)
    text_tokens = gaussian(key_list[2], (PAIRS, L, D), 1.0, 6.0, ((0, 128),))
    partner = jax.random.permutation(key_list[3], PAIRS).astype(jnp.int32)
    scale = jnp.clip(jnp.exp(jax.random.uniform(key_list[4], (1,), jnp.float32, math.log(4.0), math.log(16.0))), 4.0, 16.0)
    shift = jnp.clip(jax.random.uniform(key_list[5], (1,), jnp.float32, -6.0, -2.0), -6.0, -2.0)
    img_w_in = gaussian(key_list[6], (D, FF), D ** -0.5, 0.15625, ((0, 8), (1, 2)))
    img_w_out = gaussian(key_list[7], (FF, D), FF ** -0.5, 0.09375, ((0, 2), (1, 8)))
    txt_w_in = gaussian(key_list[8], (D, FF), D ** -0.5, 0.15625, ((0, 16), (1, 2)))
    txt_w_out = gaussian(key_list[9], (FF, D), FF ** -0.5, 0.09375, ((0, 2), (1, 16)))
    return dict(patches=patches, counts=counts, text_tokens=text_tokens, partner=partner, scale=scale, shift=shift, img_w_in=img_w_in, img_w_out=img_w_out, txt_w_in=txt_w_in, txt_w_out=txt_w_out)


def silu_grad(value):
    sig = jax.nn.sigmoid(value)
    return sig * (1.0 + value * (1.0 - sig))

def block_forward(tokens, counts, w_in, w_out):
    nb, slots, width = tokens.shape
    mask = (jnp.arange(slots)[None, :] < counts[:, None]).astype(jnp.float32)
    cnt = counts.astype(jnp.float32)[:, None]
    pre = jnp.dot(tokens.reshape(nb * slots, width), w_in, preferred_element_type=jnp.float32).reshape(nb, slots, -1)
    pooled_hidden = (lax.optimization_barrier(jnp.sum(mask[:, :, None] * jax.nn.silu(pre), 1)) / cnt).astype(jnp.bfloat16)
    pooled_x = lax.optimization_barrier(jnp.sum(mask[:, :, None] * tokens.astype(jnp.float32), 1)) / cnt
    return pooled_x + jnp.dot(pooled_hidden, w_out, preferred_element_type=jnp.float32)

def block_backward(tokens, counts, dpooled, w_in, w_out):
    nb, slots, width = tokens.shape
    mask = (jnp.arange(slots)[None, :] < counts[:, None]).astype(jnp.float32)
    cnt = counts.astype(jnp.float32)[:, None]
    pre = jnp.dot(tokens.reshape(nb * slots, width), w_in, preferred_element_type=jnp.float32).reshape(nb, slots, -1)
    dtoken = dpooled / cnt
    dhidden = jnp.dot(dtoken.astype(jnp.bfloat16), w_out.T, preferred_element_type=jnp.float32)
    dpre = (mask[:, :, None] * dhidden[:, None, :] * silu_grad(pre)).astype(jnp.bfloat16)
    back = jnp.dot(dpre.reshape(nb * slots, -1), w_in.T, preferred_element_type=jnp.float32).reshape(nb, slots, width)
    return (mask[:, :, None] * dtoken[:, None, :] + back).astype(jnp.bfloat16)

def tower_pooled(tokens, counts, w_in, w_out):
    slots, width = (tokens.shape[1], tokens.shape[2])
    groups = tokens.reshape(-1, 16, slots, width)
    cgroups = counts.reshape(-1, 16)
    out = lax.map(lambda item: block_forward(item[0], item[1], w_in, w_out), (groups, cgroups))
    return out.reshape(-1, width)

def tower_grad(tokens, counts, dpooled, w_in, w_out):
    slots, width = (tokens.shape[1], tokens.shape[2])
    groups = tokens.reshape(-1, 16, slots, width)
    cgroups = counts.reshape(-1, 16)
    dgroups = dpooled.reshape(-1, 16, width)
    out = lax.map(lambda item: block_backward(item[0], item[1], item[2], w_in, w_out), (groups, cgroups, dgroups))
    return out.reshape(tokens.shape)

def reference(patches, counts, text_tokens, partner, scale, shift, img_w_in, img_w_out, txt_w_in, txt_w_out):
    text_counts = jnp.full((PAIRS,), L, jnp.int32)
    pooled_img = tower_pooled(patches, counts, img_w_in, img_w_out)
    pooled_txt = tower_pooled(text_tokens, text_counts, txt_w_in, txt_w_out)
    norm_img = jnp.sqrt(lax.optimization_barrier(jnp.sum(pooled_img * pooled_img, -1, keepdims=True)) + 1e-06)
    norm_txt = jnp.sqrt(lax.optimization_barrier(jnp.sum(pooled_txt * pooled_txt, -1, keepdims=True)) + 1e-06)
    emb_img = pooled_img / norm_img
    emb_txt = pooled_txt / norm_txt
    temp = scale[0]
    logits = temp * jnp.dot(emb_img, emb_txt.T, precision=lax.Precision.HIGHEST) + shift[0]
    sign = jnp.where(partner[:, None] == jnp.arange(PAIRS, dtype=jnp.int32)[None, :], 1.0, -1.0)
    dlogits = -sign * jax.nn.sigmoid(-sign * logits)
    d_img = temp * jnp.dot(dlogits, emb_txt, precision=lax.Precision.HIGHEST)
    d_txt = temp * jnp.dot(dlogits.T, emb_img, precision=lax.Precision.HIGHEST)
    dp_img = (d_img - emb_img * lax.optimization_barrier(jnp.sum(emb_img * d_img, -1, keepdims=True))) / norm_img
    dp_txt = (d_txt - emb_txt * lax.optimization_barrier(jnp.sum(emb_txt * d_txt, -1, keepdims=True))) / norm_txt
    grad_patches = tower_grad(patches, counts, dp_img, img_w_in, img_w_out)
    grad_text = tower_grad(text_tokens, text_counts, dp_txt, txt_w_in, txt_w_out)
    return (grad_patches, grad_text)
```

```python
import jax
import jax.numpy as jnp
from jax import lax
from jax.experimental import pallas as pl
from jax.experimental.pallas import tpu as pltpu
from jax.sharding import PartitionSpec as P

F32, BF16 = jnp.float32, jnp.bfloat16
TXT, IMG = 0, 1
NROW, NCOL, SIDE = 16, 8, 4
D, HID, HALF, PAD = 1536, 2048, 768, 2048
IPD, SLOTS, TOKENS = 4, 128, 64
MI, MT = IPD * SLOTS, IPD * TOKENS
PX, AA, CC, EE, FF = range(5)
NT = (((1,), (1,)), ((), ()))


def mm(a, b):
    return jnp.dot(a, b, preferred_element_type=F32)


def mm_nt(a, b):
    return lax.dot_general(a, b, NT, preferred_element_type=F32)


def split(v):
    hi = v.astype(BF16)
    return hi, (v - hi.astype(F32)).astype(BF16)


def kernel(
    counts, partner, scale, shift, xi_h, xt_h, wii_h, woi_h, wit_h, wot_h,
    oi_h, ot_h,
    wi, wt, xi, xt, woi_raw, wot_raw, woi, wot, sel,
    sp_i, sp_t, hp_i, hp_t, acc_i, acc_t, dpre_i, dpre_t, out_i, out_t,
    px_i, px_t, pxall_i, pxall_t, a_i, a_t, stage, ph,
    bs_i, bs_t, br_i, br_t, c_i, c_t, pool_i, pool_t,
    es_i, es_t, e_i, e_t, fs_i, fs_t, f_i, f_t, tail, f2s, f2r, dh_i, dh_t, dtp,
    gs, gr, zs, zr, ls, ms, mr, bs, br,
):
    r, c, t = lax.axis_index("row"), lax.axis_index("col"), lax.axis_index("tp")
    x, y = lax.div(r, SIDE), lax.rem(r, SIDE)
    zlo, k = lax.div(c, 2), lax.rem(c, 2)
    u = 1 - t
    pf = x * (1 - k) + y * k
    qf = y * (1 - k) + x * k
    am, bm = 4 - 3 * k, 1 + 3 * k

    def row_of(f, q):
        return f * am + q * bm

    def turn(v, by):
        return lax.rem(v + by, SIDE)

    def remote(src, dst, ssem, rsem, dev):
        return pltpu.make_async_remote_copy(
            src_ref=src, dst_ref=dst, send_sem=ssem, recv_sem=rsem,
            device_id=dev, device_id_type=pl.DeviceIdType.MESH,
        )

    own_cols = pl.ds(pl.multiple_of(128 * r, 128), 128)
    own_rows = pl.ds(pl.multiple_of(48 * k, 16), 48)

    locals_ = [
        pltpu.make_async_copy(wit_h.at[own_rows], wt.at[t, r, k], ls.at[0]),
        pltpu.make_async_copy(wii_h.at[:, own_cols], wi.at[t, r, zlo, k], ls.at[1]),
        pltpu.make_async_copy(xi_h, xi, ls.at[2]),
        pltpu.make_async_copy(xt_h, xt, ls.at[3]),
        pltpu.make_async_copy(woi_h, woi_raw, ls.at[4]),
        pltpu.make_async_copy(wot_h, wot_raw, ls.at[5]),
    ]
    for copy in locals_:
        copy.start()

    barrier = pltpu.get_barrier_semaphore()

    def greet(dev):
        pl.semaphore_signal(barrier, inc=1, device_id=dev, device_id_type=pl.DeviceIdType.MESH)

    @pl.loop(1, NCOL)
    def _(i):
        greet({"col": lax.rem(c + i, NCOL)})

    @pl.loop(1, NROW)
    def _(i):
        greet({"row": lax.rem(r + i, NROW)})

    @pl.loop(0, SIDE)
    def _(i):
        greet({"col": 2 * turn(zlo, i) + k, "tp": u})

    pl.semaphore_wait(barrier, 7 + 15 + 4)

    def z_img_same(i, slot):
        return remote(
            wii_h.at[:, own_cols], wi.at[t, r, slot, k], zs.at[i], zr.at[i], {"col": 2 * turn(zlo, i) + k}
        )

    def z_img_other(i, half, slot):
        return remote(
            wii_h.at[:, own_cols], wi.at[half, r, slot, k], zs.at[4 + i], zr.at[4 + i],
            {"col": 2 * turn(zlo, i) + k, "tp": u},
        )

    def z_txt(half):
        return remote(wit_h.at[own_rows], wt.at[half, r, k], zs.at[8], zr.at[8], {"tp": u})

    @pl.loop(1, SIDE)
    def _(i):
        z_img_same(i, zlo).start()

    def z_later():
        z_txt(t).start()

        @pl.loop(0, SIDE)
        def _(i):
            z_img_other(i, t, zlo).start()

    dev_p = [{"row": row_of(turn(pf, 1), qf)}, {"row": row_of(turn(pf, 3), qf)}]
    dev_q = [{"row": row_of(pf, turn(qf, 1))}, {"row": row_of(pf, turn(qf, 3))}]
    sibling = {"col": c + 1 - 2 * k}

    class Batch:
        def __init__(self, n, tower, half):
            self.n, self.tower, self.half = n, tower, half

        def shard(self, row, core=None):
            core = k if core is None else core
            if self.tower == TXT:
                return wt.at[self.half, row, core]
            return wi.at[self.half, row, :, core]

        def part(self, row, h):
            if self.tower == TXT:
                return wt.at[self.half, row, k, :, pl.ds(1024 * h, 1024)]
            return wi.at[self.half, row, pl.ds(2 * h, 2), k]

        def copy(self, index, ref, dev):
            return remote(ref, ref, gs.at[self.n, index], gr.at[self.n, index], dev)

        def to_sibling(self, row):
            self.copy(16 + row, self.shard(row), sibling).start()

        def spread(self, j):
            row = row_of(turn(pf, j), qf)
            ref = self.shard(row)
            self.copy(4 + 2 * j, ref, dev_q[0]).start()
            self.copy(5 + 2 * j, ref, dev_q[1]).start()
            self.to_sibling(row)

        def s1(self):
            ref = self.shard(r)
            self.copy(0, ref, dev_p[0]).start()
            self.copy(1, ref, dev_p[1]).start()
            self.spread(0)

        def s2(self):
            left, right = row_of(turn(pf, 3), qf), row_of(turn(pf, 1), qf)
            self.copy(0, self.shard(left), dev_p[0]).wait_recv()
            self.copy(2, self.part(left, 0), dev_p[0]).start()
            self.copy(1, self.shard(right), dev_p[1]).wait_recv()
            self.copy(3, self.part(right, 1), dev_p[1]).start()
            self.spread(3)
            self.spread(1)

        def s2b(self):
            far = row_of(turn(pf, 2), qf)
            self.copy(2, self.part(far, 0), dev_p[0]).wait_recv()
            self.copy(3, self.part(far, 1), dev_p[1]).wait_recv()
            self.spread(2)

        def s3(self):
            for j in (0, 3, 1, 2):
                for way, at in ((0, 3), (1, 1)):
                    row = row_of(turn(pf, j), turn(qf, at))
                    ref = self.shard(row)
                    self.copy(4 + 2 * j + way, ref, dev_q[way]).wait_recv()
                    if (j in (0, 1)) == (way == 0):
                        self.copy(12 + j, ref, dev_q[way]).start()
                    self.to_sibling(row)

        def s4(self):
            for j in (0, 3, 1, 2):
                row = row_of(turn(pf, j), turn(qf, 2))
                self.copy(12 + j, self.shard(row), dev_q[0]).wait_recv()
                self.to_sibling(row)

        def from_sibling(self):
            @pl.loop(0, NROW)
            def _(row):
                self.copy(16 + row, self.shard(row, 1 - k), sibling).wait_recv()

        def drain(self):
            for j in (0, 1):
                self.copy(j, self.shard(r), dev_p[j]).wait_send()
                self.copy(2 + j, self.part(r, j), dev_p[j]).wait_send()

            @pl.loop(4, 32)
            def _(i):
                self.copy(i, self.shard(r), dev_q[0]).wait_send()

    t0, i0, t1, i1 = Batch(0, TXT, t), Batch(1, IMG, t), Batch(2, TXT, u), Batch(3, IMG, u)

    def send_img(stage_id, src, dst):
        @pl.loop(1, NCOL)
        def _(i):
            to = lax.rem(c + i, NCOL)
            remote(src(to), dst.at[c], ms.at[stage_id, i], mr.at[stage_id, i], {"col": to}).start()

    def send_txt(stage_id, src, dst):
        @pl.loop(1, NROW)
        def _(i):
            to = lax.rem(r + i, NROW)
            remote(src(to), dst.at[r], ms.at[stage_id, 8 + i], mr.at[stage_id, 8 + i], {"row": to}).start()

    def recv_img(stage_id, dst):
        @pl.loop(1, NCOL)
        def _(i):
            ref = dst.at[lax.rem(c + NCOL - i, NCOL)]
            remote(ref, ref, ms.at[stage_id, i], mr.at[stage_id, i], {"col": lax.rem(c + i, NCOL)}).wait_recv()

    def recv_txt(stage_id, dst):
        @pl.loop(1, NROW)
        def _(i):
            ref = dst.at[lax.rem(r + NROW - i, NROW)]
            remote(ref, ref, ms.at[stage_id, 8 + i], mr.at[stage_id, 8 + i], {"row": lax.rem(r + i, NROW)}).wait_recv()

    def drain_small(stage_id, src_i, src_t):
        @pl.loop(1, NCOL)
        def _(i):
            remote(src_i.at[c], src_i.at[c], ms.at[stage_id, i], mr.at[stage_id, i], {"col": lax.rem(c + i, NCOL)}).wait_send()

        @pl.loop(1, NROW)
        def _(i):
            remote(
                src_t.at[r], src_t.at[r], ms.at[stage_id, 8 + i], mr.at[stage_id, 8 + i], {"row": lax.rem(r + i, NROW)}
            ).wait_send()

    def live(i, width):
        return lax.broadcasted_iota(jnp.int32, (SLOTS, width), 0) < counts[i]

    def counted(i, width):
        return jnp.full((1, width), counts[i], jnp.int32).astype(F32)

    def local_part():
        d = lax.broadcasted_iota(jnp.int32, (384, 512), 0)
        e = lax.broadcasted_iota(jnp.int32, (384, 512), 1)
        hit = ((e & 127) < 96) & (d == (e >> 7) * 96 + (e & 127))
        sel[...] = jnp.where(hit, 1.0, 0.0).astype(BF16)
        for copy in locals_[2:]:
            copy.wait()
        row = lax.broadcasted_iota(jnp.int32, (8, MI), 0)
        tok = lax.broadcasted_iota(jnp.int32, (8, MI), 1)
        limit = jnp.zeros((8, MI), jnp.int32)
        for i in range(IPD):
            limit = jnp.where(row == i, counts[i], limit)
        mask_i = jnp.where((tok >= SLOTS * row) & (tok < SLOTS * row + limit), 1.0, 0.0).astype(BF16)
        row = lax.broadcasted_iota(jnp.int32, (8, MT), 0)
        tok = lax.broadcasted_iota(jnp.int32, (8, MT), 1)
        mask_t = jnp.where((tok >= TOKENS * row) & (tok < TOKENS * row + TOKENS), 1.0, 0.0).astype(BF16)
        sub = lax.broadcasted_iota(jnp.int32, (8, 128), 0)
        cnt = jnp.full((8, 128), 1, jnp.int32)
        for i in range(IPD):
            cnt = jnp.where(sub == i, counts[i], cnt)
        cnt = cnt.astype(F32)
        px_i[c, :, PAD:] = cnt[0:IPD]
        sums_i = mm(mask_i, xi[...]) / cnt[:, 0:1]
        sums_t = mm(mask_t, xt[...]) / float(TOKENS)
        for sums, dst, at in ((sums_i, px_i, c), (sums_t, px_t, r)):
            hi, lo = split(sums)
            both = jnp.concatenate([hi.astype(F32), lo.astype(F32)], axis=0).astype(BF16)
            for g in range(4):
                wide = mm(both[:, 384 * g:384 * (g + 1)], sel[...])
                dst[at, :, 512 * g:512 * (g + 1)] = (wide[0:8] + wide[8:16])[0:IPD]
        send_img(PX, lambda to: px_i.at[c], px_i)
        send_txt(PX, lambda to: px_t.at[r], px_t)

    def pad_out():
        woi[...] = mm(woi_raw[...], jnp.concatenate([sel[0:192, 0:128], sel[0:192, 128:256]], axis=1)).astype(BF16)
        wot[...] = mm(wot_raw[...], sel[0:96, 0:128]).astype(BF16)
        acc_i[...] = jnp.zeros_like(acc_i)
        acc_t[...] = jnp.zeros_like(acc_t)

    def fwd_img(half, pooled):
        @pl.loop(0, 8)
        def _(p):
            w = jnp.concatenate([wi[half, 2 * p + j].reshape(D, 128) for j in (0, 1)], axis=1)
            pre = mm(xi[...], w)
            for i in range(IPD):
                v = 0.5 * pre[SLOTS * i:SLOTS * (i + 1)]
                th = jnp.tanh(v)
                on = live(i, 256)
                slope = 0.5 * (1.0 + th) * (1.0 + v * (1.0 - th))
                sp_i[half, p, SLOTS * i:SLOTS * (i + 1), :] = jnp.where(on, slope, 0.0)
                if pooled:
                    total = jnp.sum(jnp.where(on, v + v * th, 0.0), axis=0, keepdims=True)
                    hp_i[p, i:i + 1, :] = total / counted(i, 256)

    def fwd_txt(half, pooled):
        @pl.loop(0, 4)
        def _(n):
            w = wt[half, :, :, :, pl.ds(pl.multiple_of(512 * n, 512), 512)].reshape(D, 512)
            pre = mm(xt[...], w)
            for i in range(IPD):
                v = 0.5 * pre[TOKENS * i:TOKENS * (i + 1)]
                th = jnp.tanh(v)
                sp_t[half, n, TOKENS * i:TOKENS * (i + 1), :] = 0.5 * (1.0 + th) * (1.0 + v * (1.0 - th))
                if pooled:
                    hp_t[n, i:i + 1, :] = jnp.sum(v + v * th, axis=0, keepdims=True) / float(TOKENS)

    def send_hidden_img():
        for q in range(4):
            for h in range(2):
                stage[4 * q:4 * q + 4, 256 * h:256 * (h + 1)] = hp_i[2 * q + h, 0:IPD]
        a_i[c] = stage[...].astype(BF16)
        send_img(AA, lambda to: a_i.at[c], a_i)

    def send_hidden_txt():
        for q in range(4):
            stage[4 * q:4 * q + 4, :] = hp_t[q, 0:IPD]
        a_t[r] = stage[...].astype(BF16)
        send_txt(AA, lambda to: a_t.at[r], a_t)

    def projected(src, peers, w):
        for p in range(peers):
            block = src[p].astype(F32)
            for q in range(4):
                ph[4 * p:4 * p + 4, 512 * q:512 * (q + 1)] = block[4 * q:4 * q + 4]
        return mm(ph[0:4 * peers].astype(BF16), w[...])

    def to_partner(index, src, dst):
        return remote(src, dst, bs.at[index], br.at[index], {"tp": u})

    def norm_of(pool):
        inv = lax.rsqrt(jnp.sum(pool * pool, axis=-1, keepdims=True) + 1e-6)
        return pool * inv, inv

    def loss():
        for p in range(NCOL):
            pxall_i[4 * p:4 * p + 4, :] = px_i[p]
        for p in range(NROW):
            pxall_t[4 * p:4 * p + 4, :] = px_t[p]
        for p in range(NCOL):
            at = slice(256 * p, 256 * (p + 1))
            pool_i[:, at] = pxall_i[:, at] + c_i[p].astype(F32)
        for p in range(NROW):
            at = slice(128 * p, 128 * (p + 1))
            pool_t[:, at] = pxall_t[:, at] + c_t[p].astype(F32)
        emb_i, inv_i = norm_of(pool_i[...])
        emb_t, inv_t = norm_of(pool_t[...])
        ih, il = split(emb_i)
        th, tl = split(emb_t)
        ni, nt = 32, 64
        one = mm_nt(jnp.concatenate([ih, il], axis=0), th)
        cos = one[0:ni] + one[ni:] + mm_nt(ih, tl)
        two = mm_nt(jnp.concatenate([th, tl], axis=0), ih)
        cos_t = two[0:nt] + two[nt:] + mm_nt(th, il)
        temp, bias = scale[0], shift[0]
        row = lax.broadcasted_iota(jnp.int32, (ni, nt), 0)
        lane = lax.broadcasted_iota(jnp.int32, (nt, ni), 1)
        mate = jnp.zeros((ni, nt), jnp.int32)
        mate_t = jnp.zeros((nt, ni), jnp.int32)
        for i in range(ni):
            text = partner[r * ni + i]
            mate = jnp.where(row == i, text, mate)
            mate_t = jnp.where(lane == i, text, mate_t)

        def slopes(value, other, ids):
            sign = jnp.where(other == ids, 1.0, -1.0)
            return -sign * jax.nn.sigmoid(-sign * (temp * value + bias))

        dl = slopes(cos, mate, c * nt + lax.broadcasted_iota(jnp.int32, (ni, nt), 1))
        dl_t = slopes(cos_t, mate_t, c * nt + lax.broadcasted_iota(jnp.int32, (nt, ni), 0))
        dh, dlo = split(dl)
        one = mm(jnp.concatenate([dh, dlo], axis=0), th)
        g_i = one[0:ni] + one[ni:] + mm(dh, tl)
        dh, dlo = split(dl_t)
        two = mm(jnp.concatenate([dh, dlo], axis=0), ih)
        g_t = two[0:nt] + two[nt:] + mm(dh, il)
        q_i = jnp.sum(dl * cos, axis=-1, keepdims=True)
        q_t = jnp.sum(dl_t * cos_t, axis=-1, keepdims=True)
        part_i = (g_i - emb_i * q_i) * (temp * inv_i / pxall_i[:, PAD:PAD + 1])
        part_t = (g_t - emb_t * q_t) * (temp * inv_t * (1.0 / TOKENS))
        for p in range(NCOL):
            es_i[p] = part_i[:, 256 * p:256 * (p + 1)].astype(BF16)
        for p in range(NROW):
            es_t[p] = part_t[:, 128 * p:128 * (p + 1)].astype(BF16)
        e_i[c] = es_i[c]
        e_t[r] = es_t[r]
        send_img(EE, lambda to: es_i.at[to], e_i)
        send_txt(EE, lambda to: es_t.at[to], e_t)

    def dhidden(src, peers, w, dst, wide):
        total = src[0].astype(F32)
        for p in range(1, peers):
            total = total + src[p].astype(F32)
        hi, lo = split(total)
        hidden = mm_nt(hi, w[...])
        hi, lo = hi.astype(F32), lo.astype(F32)
        for p in range(peers):
            rows = slice(4 * p, 4 * p + 4)
            for q in range(4):
                stage[4 * q:4 * q + 4, :] = hidden[rows, 512 * q:512 * (q + 1)]
            dst[p, :, 0:512] = stage[...].astype(BF16)
            tail[0:4, :] = hi[rows, 0:128]
            tail[8:12, :] = lo[rows, 0:128]
            if wide:
                tail[4:8, :] = hi[rows, 128:256]
                tail[12:16, :] = lo[rows, 128:256]
            dst[p, :, 512:640] = tail[...].astype(BF16)

    def hidden_sum(src, peers, dst):
        total = src[0, :, 0:512].astype(F32)
        for p in range(1, peers):
            total = total + src[p, :, 0:512].astype(F32)
        stage[...] = total
        for q in range(4):
            dst[4 * t + q, 0:IPD, :] = stage[4 * q:4 * q + 4, :]
        return total.astype(BF16)

    def hidden_other(src, dst):
        stage[...] = src.astype(F32)
        for q in range(4):
            dst[4 * u + q, 0:IPD, :] = stage[4 * q:4 * q + 4, :]

    def back_img(half):
        @pl.loop(0, 4)
        def _(n):
            for h in range(2):
                for i in range(IPD):
                    at = slice(SLOTS * i, SLOTS * (i + 1))
                    slope = sp_i[half, 2 * n + h, at, :]
                    dpre_i[at, 256 * h:256 * (h + 1)] = (
                        slope * dh_i[4 * half + n, i:i + 1, 256 * h:256 * (h + 1)]
                    ).astype(BF16)
            w = jnp.concatenate([wi[half, 4 * n + j, pl.ds(2 * t, 2)].reshape(HALF, 128) for j in range(4)], axis=1)
            acc_i[...] += mm_nt(dpre_i[...], w)

    def back_txt(half):
        @pl.loop(0, 4)
        def _(n):
            for i in range(IPD):
                at = slice(TOKENS * i, TOKENS * (i + 1))
                dpre_t[at, :] = (sp_t[half, n, at, :] * dh_t[4 * half + n, i:i + 1, :]).astype(BF16)
            w = wt[half, pl.ds(8 * t, 8), :, :, pl.ds(pl.multiple_of(512 * n, 512), 512)].reshape(HALF, 512)
            acc_t[...] += mm_nt(dpre_t[...], w)

    def token_part(src, wide):
        if wide:
            for p in range(4):
                block = src[4 * t + p, :, 512:640].astype(F32)
                for h in range(2):
                    at = slice(256 * p + 128 * h, 256 * p + 128 * (h + 1))
                    dtp[0:4, at] = block[4 * h:4 * h + 4]
                    dtp[8:12, at] = block[8 + 4 * h:12 + 4 * h]
        else:
            for p in range(8):
                dtp[:, 128 * p:128 * (p + 1)] = src[8 * t + p, :, 512:640].astype(F32)
        natural = [mm_nt(dtp[:, 512 * g:512 * (g + 1)].astype(BF16), sel[...]) for g in range(2)]
        natural = jnp.concatenate(natural, axis=1)
        return natural[0:8] + natural[8:16]

    def finish_txt():
        token = token_part(f_t, False)
        for i in range(IPD):
            at = slice(TOKENS * i, TOKENS * (i + 1))
            out_t[at, :] = (acc_t[at, :] + token[i:i + 1]).astype(BF16)
        copy = pltpu.make_async_copy(out_t, ot_h, ls.at[6])
        copy.start()
        return copy

    def finish_img():
        token = token_part(f_i, True)
        for i in range(IPD):
            at = slice(SLOTS * i, SLOTS * (i + 1))
            out_i[at, :] = (acc_i[at, :] + jnp.where(live(i, HALF), token[i:i + 1], 0.0)).astype(BF16)
        copy = pltpu.make_async_copy(out_i, oi_h, ls.at[7])
        copy.start()
        return copy

    def await_z_same():
        @pl.loop(1, SIDE)
        def _(i):
            z_img_same(i, turn(zlo, SIDE - i)).wait_recv()

    def await_z_other():
        @pl.loop(0, SIDE)
        def _(i):
            z_img_other(i, u, turn(zlo, SIDE - i)).wait_recv()

    locals_[0].wait()
    t0.s1()
    z_later()
    tail[...] = jnp.zeros_like(tail)
    dtp[...] = jnp.zeros_like(dtp)
    local_part()
    t0.s2()
    t0.s2b()
    locals_[1].wait()
    await_z_same()
    i0.s1()
    pad_out()
    t0.s3()
    i0.s2()
    t0.s4()
    i0.s2b()
    t0.from_sibling()
    fwd_txt(t, True)
    send_hidden_txt()
    i0.s3()
    z_txt(u).wait_recv()
    t1.s1()
    i0.s4()
    t1.s2()
    t1.s2b()
    await_z_other()
    i1.s1()
    i0.from_sibling()
    fwd_img(t, True)
    send_hidden_img()
    recv_txt(AA, a_t)
    bs_t[...] = projected(a_t, NROW, wot)
    to_partner(1, bs_t, br_t).start()
    recv_img(AA, a_i)
    bs_i[...] = projected(a_i, NCOL, woi)
    to_partner(0, bs_i, br_i).start()
    i1.s2()
    to_partner(1, bs_t, br_t).wait_recv()
    c_t[r] = (bs_t[...] + br_t[...]).astype(BF16)
    send_txt(CC, lambda to: c_t.at[r], c_t)
    to_partner(0, bs_i, br_i).wait_recv()
    c_i[c] = (bs_i[...] + br_i[...]).astype(BF16)
    send_img(CC, lambda to: c_i.at[c], c_i)
    t1.s3()
    i1.s2b()
    recv_img(PX, px_i)
    recv_txt(PX, px_t)
    recv_img(CC, c_i)
    recv_txt(CC, c_t)
    loss()
    t1.s4()
    recv_img(EE, e_i)
    dhidden(e_i, NCOL, woi, fs_i, True)
    f_i[c] = fs_i[c]
    send_img(FF, lambda to: fs_i.at[to], f_i)
    recv_txt(EE, e_t)
    dhidden(e_t, NROW, wot, fs_t, False)
    f_t[r] = fs_t[r]
    send_txt(FF, lambda to: fs_t.at[to], f_t)
    i1.s3()
    recv_img(FF, f_i)
    f2s[0:16, :] = hidden_sum(f_i, NCOL, dh_i)
    recv_txt(FF, f_t)
    f2s[16:32, :] = hidden_sum(f_t, NROW, dh_t)
    to_partner(2, f2s, f2r).start()
    back_txt(t)
    i1.s4()
    back_img(t)
    t1.from_sibling()
    fwd_txt(u, False)
    to_partner(2, f2s, f2r).wait_recv()
    hidden_other(f2r[0:16, :], dh_i)
    hidden_other(f2r[16:32, :], dh_t)
    back_txt(u)
    done_t = finish_txt()
    i1.from_sibling()
    fwd_img(u, False)
    back_img(u)
    done_i = finish_img()

    @pl.loop(1, SIDE)
    def _(i):
        z_img_same(i, zlo).wait_send()

    @pl.loop(0, SIDE)
    def _(i):
        z_img_other(i, t, zlo).wait_send()

    z_txt(t).wait_send()
    for batch in (t0, i0, t1, i1):
        batch.drain()
    to_partner(0, bs_i, br_i).wait_send()
    to_partner(1, bs_t, br_t).wait_send()
    to_partner(2, f2s, f2r).wait_send()
    drain_small(PX, px_i, px_t)
    drain_small(AA, a_i, a_t)
    drain_small(CC, c_i, c_t)
    drain_small(EE, es_i, es_t)
    drain_small(FF, fs_i, fs_t)
    done_t.wait()
    done_i.wait()


def vm(*shape, dtype=F32):
    return pltpu.VMEM(shape, dtype)


SCRATCH = [
    vm(2, NROW, 4, 2, 192, 128, dtype=BF16), vm(2, NROW, 2, 48, HID, dtype=BF16),
    vm(MI, D, dtype=BF16), vm(MT, D, dtype=BF16),
    vm(HID, 192, dtype=BF16), vm(HID, 96, dtype=BF16), vm(HID, 256, dtype=BF16), vm(HID, 128, dtype=BF16),
    vm(384, 512, dtype=BF16),
    vm(2, 8, MI, 256), vm(2, 4, MT, 512), vm(8, 8, 256), vm(4, 8, 512),
    vm(MI, HALF), vm(MT, HALF), vm(MI, 512, dtype=BF16), vm(MT, 512, dtype=BF16),
    vm(MI, HALF, dtype=BF16), vm(MT, HALF, dtype=BF16),
    vm(NCOL, IPD, PAD + 128), vm(NROW, IPD, PAD), vm(32, PAD + 128), vm(64, PAD),
    vm(NCOL, 16, 512, dtype=BF16), vm(NROW, 16, 512, dtype=BF16), vm(16, 512), vm(64, HID),
    vm(32, 256), vm(64, 128), vm(32, 256), vm(64, 128),
    vm(NCOL, 32, 256, dtype=BF16), vm(NROW, 64, 128, dtype=BF16), vm(32, PAD), vm(64, PAD),
    vm(NCOL, 32, 256, dtype=BF16), vm(NROW, 64, 128, dtype=BF16),
    vm(NCOL, 32, 256, dtype=BF16), vm(NROW, 64, 128, dtype=BF16),
    vm(NCOL, 16, 640, dtype=BF16), vm(NROW, 16, 640, dtype=BF16),
    vm(NCOL, 16, 640, dtype=BF16), vm(NROW, 16, 640, dtype=BF16),
    vm(16, 128), vm(32, 512, dtype=BF16), vm(32, 512, dtype=BF16), vm(8, 8, 512), vm(8, 8, 512), vm(16, 1024),
    pltpu.SemaphoreType.DMA((4, 32)), pltpu.SemaphoreType.DMA((4, 32)),
    pltpu.SemaphoreType.DMA((9,)), pltpu.SemaphoreType.DMA((9,)),
    pltpu.SemaphoreType.DMA((8,)),
    pltpu.SemaphoreType.DMA((5, 24)), pltpu.SemaphoreType.DMA((5, 24)),
    pltpu.SemaphoreType.DMA((3,)), pltpu.SemaphoreType.DMA((3,)),
]


def shards(patches, counts, text, partner, scale, shift, img_w_in, img_w_out, txt_w_in, txt_w_out):
    smem = pl.BlockSpec(memory_space=pltpu.SMEM)
    hbm = pl.BlockSpec(memory_space=pl.ANY)
    grad_i, grad_t = pl.pallas_call(
        kernel,
        out_shape=(jax.ShapeDtypeStruct((MI, HALF), BF16), jax.ShapeDtypeStruct((MT, HALF), BF16)),
        in_specs=[smem] * 4 + [hbm] * 6,
        out_specs=(hbm, hbm),
        scratch_shapes=SCRATCH,
        compiler_params=pltpu.CompilerParams(
            collective_id=0, has_side_effects=True, vmem_limit_bytes=60 * 2**20
        ),
        name="towers",
    )(
        counts, partner, scale, shift, patches.reshape(MI, D), text.reshape(MT, D),
        img_w_in, img_w_out, txt_w_in, txt_w_out,
    )
    return grad_i.reshape(IPD, SLOTS, HALF), grad_t.reshape(IPD, TOKENS, HALF)


def solution(mesh):
    return jax.shard_map(
        shards,
        mesh=mesh,
        in_specs=(
            P(("row", "col"), None, None), P(("row", "col")), P(("col", "row"), None, None), P(), P(), P(),
            P("col", "tp"), P("tp", "col"), P("row", "tp"), P("tp", "row"),
        ),
        out_specs=(P(("row", "col"), None, "tp"), P(("col", "row"), None, "tp")),
        check_vma=False,
    )
```

```python
import jax
import jax.numpy as jnp
from jax import lax
from jax.experimental import pallas as pl
from jax.experimental.pallas import tpu as pltpu
from jax.sharding import PartitionSpec as P

F32, BF16 = jnp.float32, jnp.bfloat16
TXT, IMG = 0, 1
NROW, NCOL, SIDE = 16, 8, 4
D, HID, HALF, PAD = 1536, 2048, 768, 2048
IPD, SLOTS, TOKENS = 4, 128, 64
MI, MT = IPD * SLOTS, IPD * TOKENS
PX, AA, CC, EE, FF = range(5)
RHO = 32
NT = (((1,), (1,)), ((), ()))


def mm(a, b):
    return jnp.dot(a, b, preferred_element_type=F32)


def mm_nt(a, b):
    return lax.dot_general(a, b, NT, preferred_element_type=F32)


def split(v):
    hi = v.astype(BF16)
    return hi, (v - hi.astype(F32)).astype(BF16)


def kernel(
    counts, partner, scale, shift, xi_h, xt_h, wii_h, woi_h, wit_h, wot_h,
    out_i, out_t,
    wi, wz, wt, xi, xt, woi_raw, wot_raw, woi, wot, sel,
    sp_i, sp_t, hp_i, hp_t, acc_i, acc_t, dpre_i, dpre_t, dpre_i2, dpre_t2,
    px_i, px_t, pxs_i, pxs_t, pxall_i, pxall_t, a_i, a_t, stage, ph,
    bs_t, br_t, c_i, c_t, pool_i, pool_t,
    es_i, es_t, e_i, e_t, fs_i, fs_t, f_i, f_t, tail, f2s, f2r, dh_i, dh_t, dtp,
    gs, gr, zs, zr, ls, os_, ms, mr, bs, br, xs, xr,
):
    r, c, t = lax.axis_index("row"), lax.axis_index("col"), lax.axis_index("tp")
    x, y = lax.div(r, SIDE), lax.rem(r, SIDE)
    zlo, k = lax.div(c, 2), lax.rem(c, 2)
    u = 1 - t
    pf = x * (1 - k) + y * k
    qf = y * (1 - k) + x * k
    am, bm = 4 - 3 * k, 1 + 3 * k

    def row_of(f, q):
        return f * am + q * bm

    def turn(v, by):
        return lax.rem(v + by, SIDE)

    def remote(src, dst, ssem, rsem, dev):
        return pltpu.make_async_remote_copy(
            src_ref=src, dst_ref=dst, send_sem=ssem, recv_sem=rsem,
            device_id=dev, device_id_type=pl.DeviceIdType.MESH,
        )

    own_cols = pl.ds(pl.multiple_of(128 * r, 128), 128)
    own_rows = pl.ds(pl.multiple_of(48 * k, 16), 48)

    whole_rows, block_rows = pl.ds(192 - RHO, RHO), pl.ds(0, 192 - RHO)

    def own_block(i):
        cols = pl.ds(pl.multiple_of(128 * i, 128), 128)
        return pltpu.make_async_copy(wii_h.at[block_rows, cols], wi.at[t, i, 0, k, block_rows], os_.at[i])

    locals_ = [
        pltpu.make_async_copy(wit_h.at[own_rows], wt.at[t, r, k], ls.at[0]),
        pltpu.make_async_copy(wii_h.at[whole_rows], wz.at[0, k], ls.at[1]),
        pltpu.make_async_copy(xt_h, xt, ls.at[3]),
        pltpu.make_async_copy(woi_h, woi_raw, ls.at[4]),
        pltpu.make_async_copy(wot_h, wot_raw, ls.at[5]),
    ]
    for i in range(SIDE):
        span = pl.ds(pl.multiple_of(384 * turn(zlo, i), 128), 384)
        locals_.append(pltpu.make_async_copy(xi_h.at[:, span], xi.at[:, 384 * i:384 * (i + 1)], ls.at[8 + i]))
    for copy in locals_:
        copy.start()

    @pl.loop(0, NROW)
    def _(i):
        own_block(i).start()

    barrier = pltpu.get_barrier_semaphore()

    def greet(dev):
        pl.semaphore_signal(barrier, inc=1, device_id=dev, device_id_type=pl.DeviceIdType.MESH)

    @pl.loop(1, NCOL)
    def _(i):
        greet({"col": lax.rem(c + i, NCOL)})

    @pl.loop(1, NROW)
    def _(i):
        greet({"row": lax.rem(r + i, NROW)})

    @pl.loop(0, NCOL)
    def _(i):
        greet({"col": lax.rem(c + i, NCOL), "tp": u})

    pl.semaphore_wait(barrier, 7 + 15 + 8)

    def z_img_same(i, slot):
        return remote(
            wii_h.at[block_rows, own_cols], wi.at[t, r, slot, k, block_rows], zs.at[i], zr.at[i],
            {"col": 2 * turn(zlo, i) + k},
        )

    def z_img_whole(i, slot):
        return remote(
            wii_h.at[whole_rows], wz.at[slot, k], zs.at[8 + i], zr.at[8 + i], {"col": 2 * turn(zlo, i) + k}
        )

    def z_img_other(i, half, slot):
        return remote(
            wii_h.at[:, own_cols], wi.at[half, r, slot, k], zs.at[4 + i], zr.at[4 + i],
            {"col": 2 * turn(zlo, i) + k, "tp": u},
        )

    def z_txt(half, to, sem):
        return remote(wit_h.at[own_rows], wt.at[half, r, k], zs.at[sem], zr.at[8], {"col": 2 * to + k, "tp": u})

    def z_txt_each(act):
        @pl.when(zlo == 3)
        def _():
            act(z_txt(t, 0, 8))
            act(z_txt(t, 1, 0))

        @pl.when(zlo == 0)
        def _():
            act(z_txt(t, 3, 8))
            act(z_txt(t, 2, 0))

    sibling = {"col": c + 1 - 2 * k}

    def whole_to_sibling(i, core):
        ref = wz.at[i, core]
        return remote(ref, ref, zs.at[12 + i], zr.at[12 + i], sibling)

    def own_to_sibling(core):
        ref = wi.at[t, :, 0, core, block_rows]
        return remote(ref, ref, zs.at[16], zr.at[16], sibling)

    @pl.loop(1, SIDE)
    def _(i):
        z_img_same(i, SIDE - i).start()

    def z_later():
        @pl.loop(0, SIDE)
        def _(i):
            z_img_other(i, t, lax.rem(SIDE - i, SIDE)).start()

    dev_p = [{"row": row_of(turn(pf, 1), qf)}, {"row": row_of(turn(pf, 3), qf)}]
    dev_q = [{"row": row_of(pf, turn(qf, 1))}, {"row": row_of(pf, turn(qf, 3))}]
    class Batch:
        def __init__(self, n, tower, half):
            self.n, self.tower, self.half = n, tower, half
            own = n == 1
            self.first, self.rows = (1, 192 - RHO) if own else (0, 192)

        def shard(self, row, core=None):
            core = k if core is None else core
            if self.tower == TXT:
                return wt.at[self.half, row, core]
            return self.block(row, core, 0, self.rows)

        def block(self, row, core, start, rows):
            return wi.at[self.half, row, self.first:SIDE, core, pl.ds(start, rows)]

        def part(self, row, h):
            if self.tower == TXT:
                return wt.at[self.half, row, k, :, pl.ds(1024 * h, 1024)]
            return self.block(row, k, self.rows // 2 * h, self.rows // 2)

        def copy(self, index, ref, dev):
            return remote(ref, ref, gs.at[self.n, index], gr.at[self.n, index], dev)

        def to_sibling(self, row):
            self.copy(16 + row, self.shard(row), sibling).start()

        def spread(self, j):
            row = row_of(turn(pf, j), qf)
            ref = self.shard(row)
            self.copy(4 + 2 * j, ref, dev_q[0]).start()
            self.copy(5 + 2 * j, ref, dev_q[1]).start()
            self.to_sibling(row)

        def s1(self):
            ref = self.shard(r)
            self.copy(0, ref, dev_p[0]).start()
            self.copy(1, ref, dev_p[1]).start()
            self.spread(0)

        def s2(self):
            left, right = row_of(turn(pf, 3), qf), row_of(turn(pf, 1), qf)
            self.copy(0, self.shard(left), dev_p[0]).wait_recv()
            self.copy(2, self.part(left, 0), dev_p[0]).start()
            self.copy(1, self.shard(right), dev_p[1]).wait_recv()
            self.copy(3, self.part(right, 1), dev_p[1]).start()
            self.spread(3)
            self.spread(1)

        def s2b(self):
            far = row_of(turn(pf, 2), qf)
            self.copy(2, self.part(far, 0), dev_p[0]).wait_recv()
            self.copy(3, self.part(far, 1), dev_p[1]).wait_recv()
            self.spread(2)

        def s3(self, *js):
            for j in js:
                for way, at in ((0, 3), (1, 1)):
                    row = row_of(turn(pf, j), turn(qf, at))
                    ref = self.shard(row)
                    self.copy(4 + 2 * j + way, ref, dev_q[way]).wait_recv()
                    if (j in (0, 1)) == (way == 0):
                        self.copy(12 + j, ref, dev_q[way]).start()
                    self.to_sibling(row)

        def s4(self):
            for j in (0, 3, 1, 2):
                row = row_of(turn(pf, j), turn(qf, 2))
                self.copy(12 + j, self.shard(row), dev_q[0]).wait_recv()
                self.to_sibling(row)

        def from_sibling(self):
            @pl.loop(0, NROW)
            def _(row):
                self.row_from_sibling(row)

        def row_from_sibling(self, row):
            self.copy(16 + row, self.shard(row, 1 - k), sibling).wait_recv()

        def drain(self):
            for j in (0, 1):
                self.copy(j, self.shard(r), dev_p[j]).wait_send()
                self.copy(2 + j, self.part(r, j), dev_p[j]).wait_send()

            @pl.loop(4, 32)
            def _(i):
                self.copy(i, self.shard(r), dev_q[0]).wait_send()

    t0, i0, t1, i1 = Batch(0, TXT, t), Batch(1, IMG, t), Batch(2, TXT, u), Batch(3, IMG, u)

    def send_img(stage_id, src, dst):
        @pl.loop(1, NCOL)
        def _(i):
            to = lax.rem(c + i, NCOL)
            remote(src(to), dst.at[c], ms.at[stage_id, i], mr.at[stage_id, i], {"col": to}).start()

    def send_txt(stage_id, src, dst):
        @pl.loop(1, NROW)
        def _(i):
            to = lax.rem(r + i, NROW)
            remote(src(to), dst.at[r], ms.at[stage_id, 8 + i], mr.at[stage_id, 8 + i], {"row": to}).start()

    def recv_img(stage_id, dst):
        @pl.loop(1, NCOL)
        def _(i):
            ref = dst.at[lax.rem(c + NCOL - i, NCOL)]
            remote(ref, ref, ms.at[stage_id, i], mr.at[stage_id, i], {"col": lax.rem(c + i, NCOL)}).wait_recv()

    def recv_txt(stage_id, dst):
        @pl.loop(1, NROW)
        def _(i):
            ref = dst.at[lax.rem(r + NROW - i, NROW)]
            remote(ref, ref, ms.at[stage_id, 8 + i], mr.at[stage_id, 8 + i], {"row": lax.rem(r + i, NROW)}).wait_recv()

    def drain_small(stage_id, src_i, src_t):
        @pl.loop(1, NCOL)
        def _(i):
            remote(src_i.at[c], src_i.at[c], ms.at[stage_id, i], mr.at[stage_id, i], {"col": lax.rem(c + i, NCOL)}).wait_send()

        @pl.loop(1, NROW)
        def _(i):
            remote(
                src_t.at[r], src_t.at[r], ms.at[stage_id, 8 + i], mr.at[stage_id, 8 + i], {"row": lax.rem(r + i, NROW)}
            ).wait_send()

    def live(i, width):
        return lax.broadcasted_iota(jnp.int32, (SLOTS, width), 0) < counts[i]

    def counted(i, width):
        return jnp.full((1, width), counts[i], jnp.int32).astype(F32)

    def local_part():
        d = lax.broadcasted_iota(jnp.int32, (384, 512), 0)
        e = lax.broadcasted_iota(jnp.int32, (384, 512), 1)
        hit = ((e & 127) < 96) & (d == (e >> 7) * 96 + (e & 127))
        sel[...] = jnp.where(hit, 1.0, 0.0).astype(BF16)
        for copy in locals_[2:]:
            copy.wait()
        row = lax.broadcasted_iota(jnp.int32, (8, MI), 0)
        tok = lax.broadcasted_iota(jnp.int32, (8, MI), 1)
        limit = jnp.zeros((8, MI), jnp.int32)
        for i in range(IPD):
            limit = jnp.where(row == i, counts[i], limit)
        mask_i = jnp.where((tok >= SLOTS * row) & (tok < SLOTS * row + limit), 1.0, 0.0).astype(BF16)
        row = lax.broadcasted_iota(jnp.int32, (8, MT), 0)
        tok = lax.broadcasted_iota(jnp.int32, (8, MT), 1)
        mask_t = jnp.where((tok >= TOKENS * row) & (tok < TOKENS * row + TOKENS), 1.0, 0.0).astype(BF16)
        sub = lax.broadcasted_iota(jnp.int32, (8, 128), 0)
        cnt = jnp.full((8, 128), 1, jnp.int32)
        for i in range(IPD):
            cnt = jnp.where(sub == i, counts[i], cnt)
        cnt = cnt.astype(F32)
        for p in range(NCOL):
            pxs_i[p, :, 256:] = cnt[0:IPD]
        sums_i = mm(mask_i, xi[...]) / cnt[:, 0:1]
        sums_t = mm(mask_t, xt[...]) / float(TOKENS)
        for sums, dst, per in ((sums_i, pxs_i, 256), (sums_t, pxs_t, 128)):
            hi, lo = split(sums)
            both = jnp.concatenate([hi.astype(F32), lo.astype(F32)], axis=0).astype(BF16)
            for g in range(4):
                wide = mm(both[:, 384 * g:384 * (g + 1)], sel[...])
                wide = (wide[0:8] + wide[8:16])[0:IPD]
                first = 2 * turn(zlo, g) if per == 256 else 4 * g
                for p in range(512 // per):
                    dst[first + p, :, 0:per] = wide[:, per * p:per * (p + 1)]
        px_i[c] = pxs_i[c]
        px_t[r] = pxs_t[r]
        send_img(PX, lambda to: pxs_i.at[to], px_i)
        send_txt(PX, lambda to: pxs_t.at[to], px_t)

    def pooled_tokens(src, peers, width, dst):
        for p in range(peers):
            dst[4 * p:4 * p + 4, :] = src[p]
        return dst[:, 0:width]

    def pad_out():
        for raw, dst, narrow, wide in ((woi_raw, woi, 192, 256), (wot_raw, wot, 96, 128)):
            e = lax.broadcasted_iota(jnp.int32, (wide, narrow), 0)
            d = lax.broadcasted_iota(jnp.int32, (wide, narrow), 1)
            hit = ((e & 127) < 96) & (d == (e >> 7) * 96 + (e & 127))
            dst[...] = mm(jnp.where(hit, 1.0, 0.0).astype(BF16), raw[...]).astype(BF16)

    def img_rows(own, half, row, ds):
        if not own:
            return jnp.concatenate([wi[half, row, d].reshape(384, 128) for d in ds], axis=0)
        cols = pl.ds(pl.multiple_of(128 * row, 128), 128)
        return jnp.concatenate(
            [v for d in ds for h in (0, 1) for v in (wi[half, row, d, h, block_rows], wz[d, h, :, cols])], axis=0
        )

    def img_block(own, half, p, pooled):
        w = jnp.concatenate([img_rows(own, half, 2 * p + j, range(SIDE)) for j in (0, 1)], axis=1)
        pre = mm(xi[...], w)
        for i in range(IPD):
            v = 0.5 * pre[SLOTS * i:SLOTS * (i + 1)]
            th = jnp.tanh(v)
            on = live(i, 256)
            slope = 0.5 * (1.0 + th) * (1.0 + v * (1.0 - th))
            sp_i[half, p, SLOTS * i:SLOTS * (i + 1), :] = jnp.where(on, slope, 0.0)
            if pooled:
                total = jnp.sum(jnp.where(on, v + v * th, 0.0), axis=0, keepdims=True)
                hp_i[p, i:i + 1, :] = total / counted(i, 256)

    def fwd_img(batch, pooled, first, last):
        near = lax.div(y, 2)

        def block_of(n):
            m, e = lax.rem(n, 4), lax.div(n, 4)
            along = m + lax.div(m, 2) * (1 - 2 * lax.rem(m, 2))
            return 2 * turn(x, along) + near + e * (1 - 2 * near)

        @pl.loop(first, last)
        def _(n):
            ps = [block_of(2 * n), block_of(2 * n + 1)]
            for p in ps:
                batch.row_from_sibling(2 * p)
                batch.row_from_sibling(2 * p + 1)
            for p in ps:
                img_block(batch.n == 1, batch.half, p, pooled)

    def fwd_txt(half, pooled):
        @pl.loop(0, 4, unroll=2)
        def _(n):
            w = wt[half, :, :, :, pl.ds(pl.multiple_of(512 * n, 512), 512)].reshape(D, 512)
            pre = mm(xt[...], w)
            for i in range(IPD):
                v = 0.5 * pre[TOKENS * i:TOKENS * (i + 1)]
                th = jnp.tanh(v)
                sp_t[half, n, TOKENS * i:TOKENS * (i + 1), :] = 0.5 * (1.0 + th) * (1.0 + v * (1.0 - th))
                if pooled:
                    hp_t[n, i:i + 1, :] = jnp.sum(v + v * th, axis=0, keepdims=True) / float(TOKENS)

    def send_hidden_img():
        for q in range(4):
            for h in range(2):
                stage[4 * q:4 * q + 4, 256 * h:256 * (h + 1)] = hp_i[2 * q + h, 0:IPD]
        a_i[c] = stage[...].astype(BF16)
        send_img(AA, lambda to: a_i.at[c], a_i)

    def send_hidden_txt():
        for q in range(4):
            stage[4 * q:4 * q + 4, :] = hp_t[q, 0:IPD]
        a_t[r] = stage[...].astype(BF16)
        send_txt(AA, lambda to: a_t.at[r], a_t)

    def projected(src, peers, w):
        for p in range(peers):
            block = src[p].astype(F32)
            for q in range(4):
                ph[4 * p:4 * p + 4, 512 * q:512 * (q + 1)] = block[4 * q:4 * q + 4]
        return mm_nt(ph[0:4 * peers].astype(BF16), w[...])

    def to_partner(index, src, dst):
        return remote(src, dst, bs.at[index], br.at[index], {"tp": u})

    def to_other(i, half, slot):
        ref = c_i.at[half, slot]
        return remote(ref, ref, xs.at[i], xr.at[i], {"col": lax.rem(c + i, NCOL), "tp": u})

    def send_pooled_img():
        @pl.loop(0, NCOL)
        def _(i):
            to_other(i, t, c).start()

        send_img(CC, lambda to: c_i.at[t, c], c_i.at[t])

    def recv_pooled_img():
        @pl.loop(0, NCOL)
        def _(i):
            to_other(i, u, lax.rem(c + NCOL - i, NCOL)).wait_recv()

        recv_img(CC, c_i.at[t])

    def norm_of(pool):
        inv = lax.rsqrt(jnp.sum(pool * pool, axis=-1, keepdims=True) + 1e-6)
        return pool * inv, inv

    def loss():
        for p in range(NCOL):
            pool_i[:, 256 * p:256 * (p + 1)] = c_i[0, p].astype(F32) + c_i[1, p].astype(F32)
        for p in range(NROW):
            pool_t[:, 128 * p:128 * (p + 1)] = c_t[p].astype(F32)
        emb_i, inv_i = norm_of(pool_i[...])
        emb_t, inv_t = norm_of(pool_t[...])
        ih, il = split(emb_i)
        th, tl = split(emb_t)
        ni, nt = 32, 64
        one = mm_nt(jnp.concatenate([ih, il], axis=0), th)
        cos = one[0:ni] + one[ni:] + mm_nt(ih, tl)
        two = mm_nt(jnp.concatenate([th, tl], axis=0), ih)
        cos_t = two[0:nt] + two[nt:] + mm_nt(th, il)
        temp, bias = scale[0], shift[0]
        row = lax.broadcasted_iota(jnp.int32, (ni, nt), 0)
        lane = lax.broadcasted_iota(jnp.int32, (nt, ni), 1)
        mate = jnp.zeros((ni, nt), jnp.int32)
        mate_t = jnp.zeros((nt, ni), jnp.int32)
        for i in range(ni):
            text = partner[r * ni + i]
            mate = jnp.where(row == i, text, mate)
            mate_t = jnp.where(lane == i, text, mate_t)

        def slopes(value, other, ids):
            sign = jnp.where(other == ids, 1.0, -1.0)
            return -sign * jax.nn.sigmoid(-sign * (temp * value + bias))

        dl = slopes(cos, mate, c * nt + lax.broadcasted_iota(jnp.int32, (ni, nt), 1))
        dl_t = slopes(cos_t, mate_t, c * nt + lax.broadcasted_iota(jnp.int32, (nt, ni), 0))
        dh, dlo = split(dl)
        one = mm(jnp.concatenate([dh, dlo], axis=0), th)
        g_i = one[0:ni] + one[ni:] + mm(dh, tl)
        dh, dlo = split(dl_t)
        two = mm(jnp.concatenate([dh, dlo], axis=0), ih)
        g_t = two[0:nt] + two[nt:] + mm(dh, il)
        q_i = jnp.sum(dl * cos, axis=-1, keepdims=True)
        q_t = jnp.sum(dl_t * cos_t, axis=-1, keepdims=True)
        part_i = (g_i - emb_i * q_i) * (temp * inv_i / pxall_i[:, 256:257])
        part_t = (g_t - emb_t * q_t) * (temp * inv_t * (1.0 / TOKENS))
        for p in range(NCOL):
            es_i[p] = part_i[:, 256 * p:256 * (p + 1)].astype(BF16)
        for p in range(NROW):
            es_t[p] = part_t[:, 128 * p:128 * (p + 1)].astype(BF16)
        e_i[c] = es_i[c]
        e_t[r] = es_t[r]
        send_img(EE, lambda to: es_i.at[to], e_i)
        send_txt(EE, lambda to: es_t.at[to], e_t)

    def dhidden(src, peers, w, dst, wide):
        total = src[0].astype(F32)
        for p in range(1, peers):
            total = total + src[p].astype(F32)
        hi, lo = split(total)
        hidden = mm(hi, w[...])
        hi, lo = hi.astype(F32), lo.astype(F32)
        for p in range(peers):
            rows = slice(4 * p, 4 * p + 4)
            for q in range(4):
                stage[4 * q:4 * q + 4, :] = hidden[rows, 512 * q:512 * (q + 1)]
            dst[p, :, 0:512] = stage[...].astype(BF16)
            tail[0:4, :] = hi[rows, 0:128]
            tail[8:12, :] = lo[rows, 0:128]
            if wide:
                tail[4:8, :] = hi[rows, 128:256]
                tail[12:16, :] = lo[rows, 128:256]
            dst[p, :, 512:640] = tail[...].astype(BF16)

    def hidden_sum(src, peers, dst):
        total = src[0, :, 0:512].astype(F32)
        for p in range(1, peers):
            total = total + src[p, :, 0:512].astype(F32)
        stage[...] = total
        for q in range(4):
            dst[4 * t + q, 0:IPD, :] = stage[4 * q:4 * q + 4, :]
        return total.astype(BF16)

    def hidden_other(src, dst):
        stage[...] = src.astype(F32)
        for q in range(4):
            dst[4 * u + q, 0:IPD, :] = stage[4 * q:4 * q + 4, :]

    def back(piece, add, bufs):
        piece(0, bufs[0])
        piece(1, bufs[1])
        total = add(0, bufs[0])
        piece(2, bufs[0])
        total += add(1, bufs[1])
        piece(3, bufs[1])
        total += add(2, bufs[0])
        return total + add(3, bufs[1])

    def back_img(own, half):
        def piece(n, dst):
            for h in range(2):
                for i in range(IPD):
                    at = slice(SLOTS * i, SLOTS * (i + 1))
                    slope = sp_i[half, 2 * n + h, at, :]
                    dst[at, 256 * h:256 * (h + 1)] = (
                        slope * dh_i[4 * half + n, i:i + 1, 256 * h:256 * (h + 1)]
                    ).astype(BF16)

        def add(n, src):
            ds = [lax.rem(2 * t + j + SIDE - zlo, SIDE) for j in (0, 1)]
            w = jnp.concatenate([img_rows(own, half, 4 * n + j, ds) for j in range(4)], axis=1)
            return mm_nt(src[...], w)

        return back(piece, add, (dpre_i, dpre_i2))

    def back_txt(half):
        def piece(n, dst):
            for i in range(IPD):
                at = slice(TOKENS * i, TOKENS * (i + 1))
                dst[at, :] = (sp_t[half, n, at, :] * dh_t[4 * half + n, i:i + 1, :]).astype(BF16)

        def add(n, src):
            w = wt[half, pl.ds(8 * t, 8), :, :, pl.ds(512 * n, 512)].reshape(HALF, 512)
            return mm_nt(src[...], w)

        return back(piece, add, (dpre_t, dpre_t2))

    def token_part(src, wide):
        if wide:
            for p in range(4):
                block = src[4 * t + p, :, 512:640].astype(F32)
                for h in range(2):
                    at = slice(256 * p + 128 * h, 256 * p + 128 * (h + 1))
                    dtp[0:4, at] = block[4 * h:4 * h + 4]
                    dtp[8:12, at] = block[8 + 4 * h:12 + 4 * h]
        else:
            for p in range(8):
                dtp[:, 128 * p:128 * (p + 1)] = src[8 * t + p, :, 512:640].astype(F32)
        natural = [mm_nt(dtp[:, 512 * g:512 * (g + 1)].astype(BF16), sel[...]) for g in range(2)]
        natural = jnp.concatenate(natural, axis=1)
        return natural[0:8] + natural[8:16]

    def finish_txt():
        token = token_part(f_t, False)
        acc_t[...] += back_txt(u)
        for i in range(IPD):
            at = slice(TOKENS * i, TOKENS * (i + 1))
            out_t[at, :] = (acc_t[at, :] + token[i:i + 1]).astype(BF16)

    def finish_img():
        token = token_part(f_i, True)
        acc_i[...] += back_img(False, u)
        for i in range(IPD):
            at = slice(SLOTS * i, SLOTS * (i + 1))
            out_i[at, :] = (acc_i[at, :] + jnp.where(live(i, HALF), token[i:i + 1], 0.0)).astype(BF16)

    def await_z_same():
        @pl.loop(1, SIDE)
        def _(i):
            z_img_same(i, i).wait_recv()

    def await_z_whole():
        locals_[1].wait()
        whole_to_sibling(0, k).start()

        @pl.loop(1, SIDE)
        def _(i):
            z_img_whole(i, SIDE - i).wait_recv()
            whole_to_sibling(SIDE - i, k).start()

    def await_sibling_whole():
        own_to_sibling(1 - k).wait_recv()

        @pl.loop(0, SIDE)
        def _(i):
            whole_to_sibling(i, 1 - k).wait_recv()

    def await_z_other():
        @pl.loop(0, SIDE)
        def _(i):
            z_img_other(i, u, i).wait_recv()

    locals_[0].wait()
    t0.s1()
    z_txt_each(lambda copy: copy.start())

    @pl.loop(1, SIDE)
    def _(i):
        z_img_whole(i, SIDE - i).start()

    t0.s2()
    t0.s2b()
    await_z_same()
    i0.s1()

    @pl.loop(0, NROW)
    def _(i):
        own_block(i).wait()

    own_to_sibling(k).start()
    tail[...] = jnp.zeros_like(tail)
    dtp[...] = jnp.zeros_like(dtp)
    t0.s3(0)
    i0.s2()
    local_part()
    z_later()
    t0.s3(3, 1)
    i0.s2b()
    t0.s3(2)
    pad_out()
    t0.s4()
    i0.s3(0, 3)
    t0.from_sibling()
    fwd_txt(t, True)
    send_hidden_txt()
    await_z_whole()
    z_txt(u, zlo, 8).wait_recv()
    t1.s1()
    i0.s3(1, 2)
    recv_txt(AA, a_t)
    bs_t[...] = projected(a_t, NROW, wot)
    to_partner(1, bs_t, br_t).start()
    await_sibling_whole()
    fwd_img(i0, True, 0, 1)
    i0.s4()
    fwd_img(i0, True, 1, 2)
    t1.s2()
    to_partner(1, bs_t, br_t).wait_recv()
    recv_txt(PX, px_t)
    c_t[r] = (bs_t[...] + br_t[...] + pooled_tokens(px_t, NROW, 128, pxall_t)).astype(BF16)
    send_txt(CC, lambda to: c_t.at[r], c_t)
    fwd_img(i0, True, 2, 4)
    send_hidden_img()
    t1.s2b()
    t1.s3(0)
    recv_img(AA, a_i)
    recv_img(PX, px_i)
    tokens = jnp.where(t == 0, pooled_tokens(px_i, NCOL, 256, pxall_i), 0.0)
    c_i[t, c] = (projected(a_i, NCOL, woi) + tokens).astype(BF16)
    send_pooled_img()
    t1.s3(3, 1)
    recv_txt(CC, c_t)
    t1.s3(2)
    await_z_other()
    i1.s1()
    t1.s4()
    recv_pooled_img()
    loss()
    i1.s2()
    i1.s2b()
    t1.from_sibling()
    fwd_txt(u, False)
    i1.s3(0)
    recv_img(EE, e_i)
    dhidden(e_i, NCOL, woi, fs_i, True)
    f_i[c] = fs_i[c]
    send_img(FF, lambda to: fs_i.at[to], f_i)
    i1.s3(3)
    recv_txt(EE, e_t)
    dhidden(e_t, NROW, wot, fs_t, False)
    f_t[r] = fs_t[r]
    send_txt(FF, lambda to: fs_t.at[to], f_t)
    i1.s3(1, 2)
    fwd_img(i1, False, 0, 1)
    recv_img(FF, f_i)
    f2s[0] = hidden_sum(f_i, NCOL, dh_i)
    to_partner(2, f2s.at[0], f2r.at[0]).start()
    i1.s4()
    acc_i[...] = back_img(True, t)
    recv_txt(FF, f_t)
    f2s[1] = hidden_sum(f_t, NROW, dh_t)
    to_partner(3, f2s.at[1], f2r.at[1]).start()
    acc_t[...] = back_txt(t)
    fwd_img(i1, False, 1, 4)
    to_partner(2, f2s.at[0], f2r.at[0]).wait_recv()
    hidden_other(f2r[0], dh_i)
    finish_img()
    to_partner(3, f2s.at[1], f2r.at[1]).wait_recv()
    hidden_other(f2r[1], dh_t)
    finish_txt()

    @pl.loop(1, SIDE)
    def _(i):
        z_img_same(i, SIDE - i).wait_send()
        z_img_whole(i, SIDE - i).wait_send()

    @pl.loop(0, SIDE)
    def _(i):
        whole_to_sibling(i, k).wait_send()
        z_img_other(i, t, lax.rem(SIDE - i, SIDE)).wait_send()

    z_txt_each(lambda copy: copy.wait_send())
    own_to_sibling(k).wait_send()
    for batch in (t0, i0, t1, i1):
        batch.drain()
    @pl.loop(0, NCOL)
    def _(i):
        to_other(i, t, c).wait_send()

    to_partner(1, bs_t, br_t).wait_send()
    to_partner(2, f2s.at[0], f2r.at[0]).wait_send()
    to_partner(3, f2s.at[1], f2r.at[1]).wait_send()
    drain_small(PX, pxs_i, pxs_t)
    drain_small(AA, a_i, a_t)
    drain_small(CC, c_i.at[t], c_t)
    drain_small(EE, es_i, es_t)
    drain_small(FF, fs_i, fs_t)


def vm(*shape, dtype=F32):
    return pltpu.VMEM(shape, dtype)


SCRATCH = [
    vm(2, NROW, 4, 2, 192, 128, dtype=BF16), vm(4, 2, RHO, HID, dtype=BF16), vm(2, NROW, 2, 48, HID, dtype=BF16),
    vm(MI, D, dtype=BF16), vm(MT, D, dtype=BF16),
    vm(192, HID, dtype=BF16), vm(96, HID, dtype=BF16), vm(256, HID, dtype=BF16), vm(128, HID, dtype=BF16),
    vm(384, 512, dtype=BF16),
    vm(2, 8, MI, 256), vm(2, 4, MT, 512), vm(8, 8, 256), vm(4, 8, 512),
    vm(MI, HALF), vm(MT, HALF), vm(MI, 512, dtype=BF16), vm(MT, 512, dtype=BF16),
    vm(MI, 512, dtype=BF16), vm(MT, 512, dtype=BF16),
    vm(NCOL, IPD, 384), vm(NROW, IPD, 128), vm(NCOL, IPD, 384), vm(NROW, IPD, 128), vm(32, 384), vm(64, 128),
    vm(NCOL, 16, 512, dtype=BF16), vm(NROW, 16, 512, dtype=BF16), vm(16, 512), vm(64, HID),
    vm(64, 128), vm(64, 128),
    vm(2, NCOL, 32, 256, dtype=BF16), vm(NROW, 64, 128, dtype=BF16), vm(32, PAD), vm(64, PAD),
    vm(NCOL, 32, 256, dtype=BF16), vm(NROW, 64, 128, dtype=BF16),
    vm(NCOL, 32, 256, dtype=BF16), vm(NROW, 64, 128, dtype=BF16),
    vm(NCOL, 16, 640, dtype=BF16), vm(NROW, 16, 640, dtype=BF16),
    vm(NCOL, 16, 640, dtype=BF16), vm(NROW, 16, 640, dtype=BF16),
    vm(16, 128), vm(2, 16, 512, dtype=BF16), vm(2, 16, 512, dtype=BF16), vm(8, 8, 512), vm(8, 8, 512), vm(16, 1024),
    pltpu.SemaphoreType.DMA((4, 32)), pltpu.SemaphoreType.DMA((4, 32)),
    pltpu.SemaphoreType.DMA((17,)), pltpu.SemaphoreType.DMA((17,)),
    pltpu.SemaphoreType.DMA((12,)), pltpu.SemaphoreType.DMA((NROW,)),
    pltpu.SemaphoreType.DMA((5, 24)), pltpu.SemaphoreType.DMA((5, 24)),
    pltpu.SemaphoreType.DMA((4,)), pltpu.SemaphoreType.DMA((4,)),
    pltpu.SemaphoreType.DMA((NCOL,)), pltpu.SemaphoreType.DMA((NCOL,)),
]


def shards(patches, counts, text, partner, scale, shift, img_w_in, img_w_out, txt_w_in, txt_w_out):
    smem = pl.BlockSpec(memory_space=pltpu.SMEM)
    hbm = pl.BlockSpec(memory_space=pl.ANY)
    grad_i, grad_t = pl.pallas_call(
        kernel,
        out_shape=(pltpu.VMEM((MI, HALF), BF16), pltpu.VMEM((MT, HALF), BF16)),
        in_specs=[smem] * 4 + [hbm] * 6,
        out_specs=(pl.BlockSpec(memory_space=pltpu.VMEM),) * 2,
        scratch_shapes=SCRATCH,
        compiler_params=pltpu.CompilerParams(
            collective_id=0, has_side_effects=True, vmem_limit_bytes=58 * 2**20
        ),
        name="towers",
    )(
        counts, partner, scale, shift, patches.reshape(MI, D), text.reshape(MT, D),
        img_w_in, img_w_out.T, txt_w_in, txt_w_out.T,
    )
    return grad_i.reshape(IPD, SLOTS, HALF), grad_t.reshape(IPD, TOKENS, HALF)


def solution(mesh):
    return jax.shard_map(
        shards,
        mesh=mesh,
        in_specs=(
            P(("row", "col"), None, None), P(("row", "col")), P(("col", "row"), None, None), P(), P(), P(),
            P("col", "tp"), P("tp", "col"), P("row", "tp"), P("tp", "row"),
        ),
        out_specs=(P(("row", "col"), None, "tp"), P(("col", "row"), None, "tp")),
        check_vma=False,
    )
```

```python
import jax
import jax.numpy as jnp
from jax import lax
from jax.experimental import pallas as pl
from jax.experimental.pallas import tpu as pltpu
from jax.sharding import PartitionSpec as P

F32, BF16 = jnp.float32, jnp.bfloat16
TXT, IMG = 0, 1
NROW, NCOL, SIDE = 16, 8, 4
D, HID, HALF, PAD = 1536, 2048, 768, 2048
IPD, SLOTS, TOKENS = 4, 128, 64
MI, MT = IPD * SLOTS, IPD * TOKENS
PX, AA, CC, EE, FF = range(5)
RHO = 64
NT = (((1,), (1,)), ((), ()))


def mm(a, b):
    return jnp.dot(a, b, preferred_element_type=F32)


def mm_nt(a, b):
    return lax.dot_general(a, b, NT, preferred_element_type=F32)


def split(v):
    hi = v.astype(BF16)
    return hi, (v - hi.astype(F32)).astype(BF16)


def kernel(
    counts, partner, scale, shift, xi_h, xt_h, wii_h, woi_h, wit_h, wot_h,
    out_i, out_t,
    wi, wz, wt, xi, xt, woi_raw, wot_raw, woi, wot, sel,
    sp_i, sp_t, hp_i, hp_t, acc_i, acc_t, dpre_i, dpre_t, dpre_i2, dpre_t2,
    px_i, px_t, pxs_i, pxs_t, pxall_i, pxall_t, a_i, a_t, stage, ph,
    bs_t, br_t, c_i, c_t, pool_i, pool_t,
    es_i, es_t, e_i, e_t, fs_i, fs_t, f_i, f_t, tail, f2s, f2r, dh_i, dh_t, dtp,
    gs, gr, zs, zr, ls, os_, ms, mr, bs, br, xs, xr,
):
    r, c, t = lax.axis_index("row"), lax.axis_index("col"), lax.axis_index("tp")
    x, y = lax.div(r, SIDE), lax.rem(r, SIDE)
    zlo, k = lax.div(c, 2), lax.rem(c, 2)
    u = 1 - t
    pf = x * (1 - k) + y * k
    qf = y * (1 - k) + x * k
    am, bm = 4 - 3 * k, 1 + 3 * k

    def row_of(f, q):
        return f * am + q * bm

    def turn(v, by):
        return lax.rem(v + by, SIDE)

    def remote(src, dst, ssem, rsem, dev):
        return pltpu.make_async_remote_copy(
            src_ref=src, dst_ref=dst, send_sem=ssem, recv_sem=rsem,
            device_id=dev, device_id_type=pl.DeviceIdType.MESH,
        )

    own_cols = pl.ds(pl.multiple_of(128 * r, 128), 128)
    own_rows = pl.ds(pl.multiple_of(48 * k, 16), 48)

    whole_rows, block_rows = pl.ds(192 - RHO, RHO), pl.ds(0, 192 - RHO)

    def own_block(i):
        cols = pl.ds(pl.multiple_of(128 * i, 128), 128)
        return pltpu.make_async_copy(wii_h.at[block_rows, cols], wi.at[t, i, 0, k, block_rows], os_.at[i])

    locals_ = [
        pltpu.make_async_copy(wit_h.at[own_rows], wt.at[t, r, k], ls.at[0]),
        pltpu.make_async_copy(wii_h.at[whole_rows], wz.at[0, k], ls.at[1]),
        pltpu.make_async_copy(xt_h, xt, ls.at[3]),
        pltpu.make_async_copy(woi_h, woi_raw, ls.at[4]),
        pltpu.make_async_copy(wot_h, wot_raw, ls.at[5]),
    ]
    for i in range(SIDE):
        span = pl.ds(pl.multiple_of(384 * turn(zlo, i), 128), 384)
        locals_.append(pltpu.make_async_copy(xi_h.at[:, span], xi.at[:, 384 * i:384 * (i + 1)], ls.at[8 + i]))
    for copy in locals_:
        copy.start()

    @pl.loop(0, NROW)
    def _(i):
        own_block(i).start()

    barrier = pltpu.get_barrier_semaphore()

    def greet(dev):
        pl.semaphore_signal(barrier, inc=1, device_id=dev, device_id_type=pl.DeviceIdType.MESH)

    @pl.loop(1, NCOL)
    def _(i):
        greet({"col": lax.rem(c + i, NCOL)})

    @pl.loop(1, NROW)
    def _(i):
        greet({"row": lax.rem(r + i, NROW)})

    @pl.loop(0, NCOL)
    def _(i):
        greet({"col": lax.rem(c + i, NCOL), "tp": u})

    pl.semaphore_wait(barrier, 7 + 15 + 8)

    def z_img_same(i, slot):
        return remote(
            wii_h.at[block_rows, own_cols], wi.at[t, r, slot, k, block_rows], zs.at[i], zr.at[i],
            {"col": 2 * turn(zlo, i) + k},
        )

    def z_img_whole(i, slot):
        return remote(
            wii_h.at[whole_rows], wz.at[slot, k], zs.at[8 + i], zr.at[8 + i], {"col": 2 * turn(zlo, i) + k}
        )

    def z_img_other(i, half, slot):
        return remote(
            wii_h.at[:, own_cols], wi.at[half, r, slot, k], zs.at[4 + i], zr.at[4 + i],
            {"col": 2 * turn(zlo, i) + k, "tp": u},
        )

    def z_txt(half, to, sem):
        return remote(wit_h.at[own_rows], wt.at[half, r, k], zs.at[sem], zr.at[8], {"col": 2 * to + k, "tp": u})

    def z_txt_each(act):
        @pl.when(zlo == 3)
        def _():
            act(z_txt(t, 0, 8))
            act(z_txt(t, 1, 0))

        @pl.when(zlo == 0)
        def _():
            act(z_txt(t, 3, 8))
            act(z_txt(t, 2, 0))

    sibling = {"col": c + 1 - 2 * k}

    def whole_to_sibling(i, core):
        ref = wz.at[i, core]
        return remote(ref, ref, zs.at[12 + i], zr.at[12 + i], sibling)

    def own_to_sibling(core):
        ref = wi.at[t, :, 0, core, block_rows]
        return remote(ref, ref, zs.at[16], zr.at[16], sibling)

    @pl.loop(1, SIDE)
    def _(i):
        z_img_same(i, SIDE - i).start()

    def z_later():
        @pl.loop(0, SIDE)
        def _(i):
            z_img_other(i, t, lax.rem(SIDE - i, SIDE)).start()

    dev_p = [{"row": row_of(turn(pf, 1), qf)}, {"row": row_of(turn(pf, 3), qf)}]
    dev_q = [{"row": row_of(pf, turn(qf, 1))}, {"row": row_of(pf, turn(qf, 3))}]
    class Batch:
        def __init__(self, n, tower, half):
            self.n, self.tower, self.half = n, tower, half
            own = n == 1
            self.first, self.rows = (1, 192 - RHO) if own else (0, 192)

        def shard(self, row, core=None):
            core = k if core is None else core
            if self.tower == TXT:
                return wt.at[self.half, row, core]
            return self.block(row, core, 0, self.rows)

        def block(self, row, core, start, rows):
            return wi.at[self.half, row, self.first:SIDE, core, pl.ds(start, rows)]

        def part(self, row, h):
            if self.tower == TXT:
                return wt.at[self.half, row, k, :, pl.ds(1024 * h, 1024)]
            return self.block(row, k, self.rows // 2 * h, self.rows // 2)

        def copy(self, index, ref, dev):
            return remote(ref, ref, gs.at[self.n, index], gr.at[self.n, index], dev)

        def to_sibling(self, row):
            self.copy(16 + row, self.shard(row), sibling).start()

        def spread(self, j):
            row = row_of(turn(pf, j), qf)
            ref = self.shard(row)
            self.copy(4 + 2 * j, ref, dev_q[0]).start()
            self.copy(5 + 2 * j, ref, dev_q[1]).start()
            self.to_sibling(row)

        def s1(self):
            ref = self.shard(r)
            self.copy(0, ref, dev_p[0]).start()
            self.copy(1, ref, dev_p[1]).start()
            self.spread(0)

        def s2(self):
            left, right = row_of(turn(pf, 3), qf), row_of(turn(pf, 1), qf)
            self.copy(0, self.shard(left), dev_p[0]).wait_recv()
            self.copy(2, self.part(left, 0), dev_p[0]).start()
            self.copy(1, self.shard(right), dev_p[1]).wait_recv()
            self.copy(3, self.part(right, 1), dev_p[1]).start()
            self.spread(3)
            self.spread(1)

        def s2b(self):
            far = row_of(turn(pf, 2), qf)
            self.copy(2, self.part(far, 0), dev_p[0]).wait_recv()
            self.copy(3, self.part(far, 1), dev_p[1]).wait_recv()
            self.spread(2)

        def s3(self, *js):
            for j in js:
                for way, at in ((0, 3), (1, 1)):
                    row = row_of(turn(pf, j), turn(qf, at))
                    ref = self.shard(row)
                    self.copy(4 + 2 * j + way, ref, dev_q[way]).wait_recv()
                    if (j in (0, 1)) == (way == 0):
                        self.copy(12 + j, ref, dev_q[way]).start()
                    self.to_sibling(row)

        def s4(self):
            for j in (0, 3, 1, 2):
                row = row_of(turn(pf, j), turn(qf, 2))
                self.copy(12 + j, self.shard(row), dev_q[0]).wait_recv()
                self.to_sibling(row)

        def from_sibling(self):
            @pl.loop(0, NROW)
            def _(row):
                self.row_from_sibling(row)

        def row_from_sibling(self, row):
            self.copy(16 + row, self.shard(row, 1 - k), sibling).wait_recv()

        def drain(self):
            for j in (0, 1):
                self.copy(j, self.shard(r), dev_p[j]).wait_send()
                self.copy(2 + j, self.part(r, j), dev_p[j]).wait_send()

            @pl.loop(4, 32)
            def _(i):
                self.copy(i, self.shard(r), dev_q[0]).wait_send()

    t0, i0, t1, i1 = Batch(0, TXT, t), Batch(1, IMG, t), Batch(2, TXT, u), Batch(3, IMG, u)

    def send_img(stage_id, src, dst):
        @pl.loop(1, NCOL)
        def _(i):
            to = lax.rem(c + i, NCOL)
            remote(src(to), dst.at[c], ms.at[stage_id, i], mr.at[stage_id, i], {"col": to}).start()

    def send_txt(stage_id, src, dst):
        @pl.loop(1, NROW)
        def _(i):
            to = lax.rem(r + i, NROW)
            remote(src(to), dst.at[r], ms.at[stage_id, 8 + i], mr.at[stage_id, 8 + i], {"row": to}).start()

    def recv_img(stage_id, dst):
        @pl.loop(1, NCOL)
        def _(i):
            ref = dst.at[lax.rem(c + NCOL - i, NCOL)]
            remote(ref, ref, ms.at[stage_id, i], mr.at[stage_id, i], {"col": lax.rem(c + i, NCOL)}).wait_recv()

    def recv_txt(stage_id, dst):
        @pl.loop(1, NROW)
        def _(i):
            ref = dst.at[lax.rem(r + NROW - i, NROW)]
            remote(ref, ref, ms.at[stage_id, 8 + i], mr.at[stage_id, 8 + i], {"row": lax.rem(r + i, NROW)}).wait_recv()

    def drain_small(stage_id, src_i, src_t):
        @pl.loop(1, NCOL)
        def _(i):
            remote(src_i.at[c], src_i.at[c], ms.at[stage_id, i], mr.at[stage_id, i], {"col": lax.rem(c + i, NCOL)}).wait_send()

        @pl.loop(1, NROW)
        def _(i):
            remote(
                src_t.at[r], src_t.at[r], ms.at[stage_id, 8 + i], mr.at[stage_id, 8 + i], {"row": lax.rem(r + i, NROW)}
            ).wait_send()

    def live(i, width):
        return lax.broadcasted_iota(jnp.int32, (SLOTS, width), 0) < counts[i]

    def counted(i, width):
        return jnp.full((1, width), counts[i], jnp.int32).astype(F32)

    def local_part():
        d = lax.broadcasted_iota(jnp.int32, (384, 512), 0)
        e = lax.broadcasted_iota(jnp.int32, (384, 512), 1)
        hit = ((e & 127) < 96) & (d == (e >> 7) * 96 + (e & 127))
        sel[...] = jnp.where(hit, 1.0, 0.0).astype(BF16)
        for copy in locals_[2:]:
            copy.wait()
        row = lax.broadcasted_iota(jnp.int32, (8, MI), 0)
        tok = lax.broadcasted_iota(jnp.int32, (8, MI), 1)
        limit = jnp.zeros((8, MI), jnp.int32)
        for i in range(IPD):
            limit = jnp.where(row == i, counts[i], limit)
        mask_i = jnp.where((tok >= SLOTS * row) & (tok < SLOTS * row + limit), 1.0, 0.0).astype(BF16)
        row = lax.broadcasted_iota(jnp.int32, (8, MT), 0)
        tok = lax.broadcasted_iota(jnp.int32, (8, MT), 1)
        mask_t = jnp.where((tok >= TOKENS * row) & (tok < TOKENS * row + TOKENS), 1.0, 0.0).astype(BF16)
        sub = lax.broadcasted_iota(jnp.int32, (8, 128), 0)
        cnt = jnp.full((8, 128), 1, jnp.int32)
        for i in range(IPD):
            cnt = jnp.where(sub == i, counts[i], cnt)
        cnt = cnt.astype(F32)
        for p in range(NCOL):
            pxs_i[p, :, 256:] = cnt[0:IPD]
        sums_i = mm(mask_i, xi[...]) / cnt[:, 0:1]
        sums_t = mm(mask_t, xt[...]) / float(TOKENS)
        for sums, dst, per in ((sums_i, pxs_i, 256), (sums_t, pxs_t, 128)):
            hi, lo = split(sums)
            both = jnp.concatenate([hi.astype(F32), lo.astype(F32)], axis=0).astype(BF16)
            for g in range(4):
                wide = mm(both[:, 384 * g:384 * (g + 1)], sel[...])
                wide = (wide[0:8] + wide[8:16])[0:IPD]
                first = 2 * turn(zlo, g) if per == 256 else 4 * g
                for p in range(512 // per):
                    dst[first + p, :, 0:per] = wide[:, per * p:per * (p + 1)]
        px_i[c] = pxs_i[c]
        px_t[r] = pxs_t[r]
        send_img(PX, lambda to: pxs_i.at[to], px_i)
        send_txt(PX, lambda to: pxs_t.at[to], px_t)

    def pooled_tokens(src, peers, width, dst):
        for p in range(peers):
            dst[4 * p:4 * p + 4, :] = src[p]
        return dst[:, 0:width]

    def pad_out():
        for raw, dst, narrow, wide in ((woi_raw, woi, 192, 256), (wot_raw, wot, 96, 128)):
            e = lax.broadcasted_iota(jnp.int32, (wide, narrow), 0)
            d = lax.broadcasted_iota(jnp.int32, (wide, narrow), 1)
            hit = ((e & 127) < 96) & (d == (e >> 7) * 96 + (e & 127))
            dst[...] = mm(jnp.where(hit, 1.0, 0.0).astype(BF16), raw[...]).astype(BF16)

    def img_rows(own, half, row, ds):
        if not own:
            return jnp.concatenate([wi[half, row, d].reshape(384, 128) for d in ds], axis=0)
        cols = pl.ds(pl.multiple_of(128 * row, 128), 128)
        return jnp.concatenate(
            [v for d in ds for h in (0, 1) for v in (wi[half, row, d, h, block_rows], wz[d, h, :, cols])], axis=0
        )

    def img_block(own, half, p, pooled):
        w = jnp.concatenate([img_rows(own, half, 2 * p + j, range(SIDE)) for j in (0, 1)], axis=1)
        pre = mm(xi[...], w)
        for i in range(IPD):
            v = 0.5 * pre[SLOTS * i:SLOTS * (i + 1)]
            th = jnp.tanh(v)
            on = live(i, 256)
            slope = 0.5 * (1.0 + th) * (1.0 + v * (1.0 - th))
            sp_i[half, p, SLOTS * i:SLOTS * (i + 1), :] = jnp.where(on, slope, 0.0)
            if pooled:
                total = jnp.sum(jnp.where(on, v + v * th, 0.0), axis=0, keepdims=True)
                hp_i[p, i:i + 1, :] = total / counted(i, 256)

    def fwd_img(batch, pooled, first, last):
        near = lax.div(y, 2)

        def block_of(n):
            m, e = lax.rem(n, 4), lax.div(n, 4)
            along = m + lax.div(m, 2) * (1 - 2 * lax.rem(m, 2))
            return 2 * turn(x, along) + near + e * (1 - 2 * near)

        @pl.loop(first, last)
        def _(n):
            ps = [block_of(2 * n), block_of(2 * n + 1)]
            for p in ps:
                batch.row_from_sibling(2 * p)
                batch.row_from_sibling(2 * p + 1)
            for p in ps:
                img_block(batch.n == 1, batch.half, p, pooled)

    def fwd_txt(half, pooled):
        @pl.loop(0, 4, unroll=2)
        def _(n):
            w = wt[half, :, :, :, pl.ds(pl.multiple_of(512 * n, 512), 512)].reshape(D, 512)
            pre = mm(xt[...], w)
            for i in range(IPD):
                v = 0.5 * pre[TOKENS * i:TOKENS * (i + 1)]
                th = jnp.tanh(v)
                sp_t[half, n, TOKENS * i:TOKENS * (i + 1), :] = 0.5 * (1.0 + th) * (1.0 + v * (1.0 - th))
                if pooled:
                    hp_t[n, i:i + 1, :] = jnp.sum(v + v * th, axis=0, keepdims=True) / float(TOKENS)

    def send_hidden_img():
        for q in range(4):
            for h in range(2):
                stage[4 * q:4 * q + 4, 256 * h:256 * (h + 1)] = hp_i[2 * q + h, 0:IPD]
        a_i[c] = stage[...].astype(BF16)
        send_img(AA, lambda to: a_i.at[c], a_i)

    def send_hidden_txt():
        for q in range(4):
            stage[4 * q:4 * q + 4, :] = hp_t[q, 0:IPD]
        a_t[r] = stage[...].astype(BF16)
        send_txt(AA, lambda to: a_t.at[r], a_t)

    def projected(src, peers, w):
        for p in range(peers):
            block = src[p].astype(F32)
            for q in range(4):
                ph[4 * p:4 * p + 4, 512 * q:512 * (q + 1)] = block[4 * q:4 * q + 4]
        return mm_nt(ph[0:4 * peers].astype(BF16), w[...])

    def to_partner(index, src, dst):
        return remote(src, dst, bs.at[index], br.at[index], {"tp": u})

    def to_other(i, half, slot):
        ref = c_i.at[half, slot]
        return remote(ref, ref, xs.at[i], xr.at[i], {"col": lax.rem(c + i, NCOL), "tp": u})

    def send_pooled_img():
        @pl.loop(0, NCOL)
        def _(i):
            to_other(i, t, c).start()

        send_img(CC, lambda to: c_i.at[t, c], c_i.at[t])

    def recv_pooled_img():
        @pl.loop(0, NCOL)
        def _(i):
            to_other(i, u, lax.rem(c + NCOL - i, NCOL)).wait_recv()

        recv_img(CC, c_i.at[t])

    def norm_of(pool):
        inv = lax.rsqrt(jnp.sum(pool * pool, axis=-1, keepdims=True) + 1e-6)
        return pool * inv, inv

    def loss():
        for p in range(NCOL):
            pool_i[:, 256 * p:256 * (p + 1)] = c_i[0, p].astype(F32) + c_i[1, p].astype(F32)
        for p in range(NROW):
            pool_t[:, 128 * p:128 * (p + 1)] = c_t[p].astype(F32)
        emb_i, inv_i = norm_of(pool_i[...])
        emb_t, inv_t = norm_of(pool_t[...])
        ih, il = split(emb_i)
        th, tl = split(emb_t)
        ni, nt = 32, 64
        one = mm_nt(jnp.concatenate([ih, il], axis=0), th)
        cos = one[0:ni] + one[ni:] + mm_nt(ih, tl)
        two = mm_nt(jnp.concatenate([th, tl], axis=0), ih)
        cos_t = two[0:nt] + two[nt:] + mm_nt(th, il)
        temp, bias = scale[0], shift[0]
        row = lax.broadcasted_iota(jnp.int32, (ni, nt), 0)
        lane = lax.broadcasted_iota(jnp.int32, (nt, ni), 1)
        mate = jnp.zeros((ni, nt), jnp.int32)
        mate_t = jnp.zeros((nt, ni), jnp.int32)
        for i in range(ni):
            text = partner[r * ni + i]
            mate = jnp.where(row == i, text, mate)
            mate_t = jnp.where(lane == i, text, mate_t)

        def slopes(value, other, ids):
            sign = jnp.where(other == ids, 1.0, -1.0)
            return -sign * jax.nn.sigmoid(-sign * (temp * value + bias))

        dl = slopes(cos, mate, c * nt + lax.broadcasted_iota(jnp.int32, (ni, nt), 1))
        dl_t = slopes(cos_t, mate_t, c * nt + lax.broadcasted_iota(jnp.int32, (nt, ni), 0))
        dh, dlo = split(dl)
        one = mm(jnp.concatenate([dh, dlo], axis=0), th)
        g_i = one[0:ni] + one[ni:] + mm(dh, tl)
        dh, dlo = split(dl_t)
        two = mm(jnp.concatenate([dh, dlo], axis=0), ih)
        g_t = two[0:nt] + two[nt:] + mm(dh, il)
        q_i = jnp.sum(dl * cos, axis=-1, keepdims=True)
        q_t = jnp.sum(dl_t * cos_t, axis=-1, keepdims=True)
        part_i = (g_i - emb_i * q_i) * (temp * inv_i / pxall_i[:, 256:257])
        part_t = (g_t - emb_t * q_t) * (temp * inv_t * (1.0 / TOKENS))
        for p in range(NCOL):
            es_i[p] = part_i[:, 256 * p:256 * (p + 1)].astype(BF16)
        for p in range(NROW):
            es_t[p] = part_t[:, 128 * p:128 * (p + 1)].astype(BF16)
        e_i[c] = es_i[c]
        e_t[r] = es_t[r]
        send_txt(EE, lambda to: es_t.at[to], e_t)
        send_img(EE, lambda to: es_i.at[to], e_i)

    def dhidden(src, peers, w, dst, wide):
        total = src[0].astype(F32)
        for p in range(1, peers):
            total = total + src[p].astype(F32)
        hi, lo = split(total)
        hidden = mm(hi, w[...])
        hi, lo = hi.astype(F32), lo.astype(F32)
        for p in range(peers):
            rows = slice(4 * p, 4 * p + 4)
            for q in range(4):
                stage[4 * q:4 * q + 4, :] = hidden[rows, 512 * q:512 * (q + 1)]
            dst[p, :, 0:512] = stage[...].astype(BF16)
            tail[0:4, :] = hi[rows, 0:128]
            tail[8:12, :] = lo[rows, 0:128]
            if wide:
                tail[4:8, :] = hi[rows, 128:256]
                tail[12:16, :] = lo[rows, 128:256]
            dst[p, :, 512:640] = tail[...].astype(BF16)

    def hidden_sum(src, peers, dst):
        total = src[0, :, 0:512].astype(F32)
        for p in range(1, peers):
            total = total + src[p, :, 0:512].astype(F32)
        stage[...] = total
        for q in range(4):
            dst[4 * t + q, 0:IPD, :] = stage[4 * q:4 * q + 4, :]
        return total.astype(BF16)

    def hidden_other(src, dst):
        stage[...] = src.astype(F32)
        for q in range(4):
            dst[4 * u + q, 0:IPD, :] = stage[4 * q:4 * q + 4, :]

    def back(piece, add, bufs):
        piece(0, bufs[0])
        piece(1, bufs[1])
        total = add(0, bufs[0])
        piece(2, bufs[0])
        total += add(1, bufs[1])
        piece(3, bufs[1])
        total += add(2, bufs[0])
        return total + add(3, bufs[1])

    def back_img(own, half):
        def piece(n, dst):
            for h in range(2):
                for i in range(IPD):
                    at = slice(SLOTS * i, SLOTS * (i + 1))
                    slope = sp_i[half, 2 * n + h, at, :]
                    dst[at, 256 * h:256 * (h + 1)] = (
                        slope * dh_i[4 * half + n, i:i + 1, 256 * h:256 * (h + 1)]
                    ).astype(BF16)

        def add(n, src):
            ds = [lax.rem(2 * t + j + SIDE - zlo, SIDE) for j in (0, 1)]
            w = jnp.concatenate([img_rows(own, half, 4 * n + j, ds) for j in range(4)], axis=1)
            return mm_nt(src[...], w)

        return back(piece, add, (dpre_i, dpre_i2))

    def back_txt(half):
        def piece(n, dst):
            for i in range(IPD):
                at = slice(TOKENS * i, TOKENS * (i + 1))
                dst[at, :] = (sp_t[half, n, at, :] * dh_t[4 * half + n, i:i + 1, :]).astype(BF16)

        def add(n, src):
            w = wt[half, pl.ds(8 * t, 8), :, :, pl.ds(512 * n, 512)].reshape(HALF, 512)
            return mm_nt(src[...], w)

        return back(piece, add, (dpre_t, dpre_t2))

    def token_part(src, wide):
        if wide:
            for p in range(4):
                block = src[4 * t + p, :, 512:640].astype(F32)
                for h in range(2):
                    at = slice(256 * p + 128 * h, 256 * p + 128 * (h + 1))
                    dtp[0:4, at] = block[4 * h:4 * h + 4]
                    dtp[8:12, at] = block[8 + 4 * h:12 + 4 * h]
        else:
            for p in range(8):
                dtp[:, 128 * p:128 * (p + 1)] = src[8 * t + p, :, 512:640].astype(F32)
        natural = [mm_nt(dtp[:, 512 * g:512 * (g + 1)].astype(BF16), sel[...]) for g in range(2)]
        natural = jnp.concatenate(natural, axis=1)
        return natural[0:8] + natural[8:16]

    def finish_txt():
        token = token_part(f_t, False)
        acc_t[...] += back_txt(u)
        for i in range(IPD):
            at = slice(TOKENS * i, TOKENS * (i + 1))
            out_t[at, :] = (acc_t[at, :] + token[i:i + 1]).astype(BF16)

    def finish_img():
        token = token_part(f_i, True)
        acc_i[...] += back_img(False, u)
        for i in range(IPD):
            at = slice(SLOTS * i, SLOTS * (i + 1))
            out_i[at, :] = (acc_i[at, :] + jnp.where(live(i, HALF), token[i:i + 1], 0.0)).astype(BF16)

    def await_z_same():
        @pl.loop(1, SIDE)
        def _(i):
            z_img_same(i, i).wait_recv()

    def await_z_whole():
        locals_[1].wait()
        whole_to_sibling(0, k).start()

        @pl.loop(1, SIDE)
        def _(i):
            z_img_whole(i, SIDE - i).wait_recv()
            whole_to_sibling(SIDE - i, k).start()

    def await_sibling_whole():
        own_to_sibling(1 - k).wait_recv()

        @pl.loop(0, SIDE)
        def _(i):
            whole_to_sibling(i, 1 - k).wait_recv()

    def await_z_other():
        @pl.loop(0, SIDE)
        def _(i):
            z_img_other(i, u, i).wait_recv()

    def drain_z():
        @pl.loop(1, SIDE)
        def _(i):
            z_img_same(i, SIDE - i).wait_send()
            z_img_whole(i, SIDE - i).wait_send()

        @pl.loop(0, SIDE)
        def _(i):
            whole_to_sibling(i, k).wait_send()
            z_img_other(i, t, lax.rem(SIDE - i, SIDE)).wait_send()

        z_txt_each(lambda copy: copy.wait_send())
        own_to_sibling(k).wait_send()

    def drain_pooled():
        @pl.loop(0, NCOL)
        def _(i):
            to_other(i, t, c).wait_send()

        drain_small(CC, c_i.at[t], c_t)

    locals_[0].wait()
    t0.s1()
    z_txt_each(lambda copy: copy.start())

    @pl.loop(1, SIDE)
    def _(i):
        z_img_whole(i, SIDE - i).start()

    t0.s2()
    t0.s2b()
    await_z_same()
    i0.s1()

    @pl.loop(0, NROW)
    def _(i):
        own_block(i).wait()

    own_to_sibling(k).start()
    tail[...] = jnp.zeros_like(tail)
    dtp[...] = jnp.zeros_like(dtp)
    t0.s3(0)
    i0.s2()
    local_part()
    z_later()
    t0.s3(3, 1)
    i0.s2b()
    t0.s3(2)
    pad_out()
    t0.s4()
    i0.s3(0, 3)
    t0.from_sibling()
    fwd_txt(t, True)
    send_hidden_txt()
    await_z_whole()
    z_txt(u, zlo, 8).wait_recv()
    t1.s1()
    i0.s3(1, 2)
    recv_txt(AA, a_t)
    bs_t[...] = projected(a_t, NROW, wot)
    to_partner(1, bs_t, br_t).start()
    await_sibling_whole()
    fwd_img(i0, True, 0, 1)
    i0.s4()
    fwd_img(i0, True, 1, 2)
    t1.s2()
    to_partner(1, bs_t, br_t).wait_recv()
    recv_txt(PX, px_t)
    c_t[r] = (bs_t[...] + br_t[...] + pooled_tokens(px_t, NROW, 128, pxall_t)).astype(BF16)
    send_txt(CC, lambda to: c_t.at[r], c_t)
    fwd_img(i0, True, 2, 4)
    send_hidden_img()
    t1.s2b()
    t1.s3(0)
    t0.drain()
    i0.drain()
    recv_img(AA, a_i)
    recv_img(PX, px_i)
    tokens = jnp.where(t == 0, pooled_tokens(px_i, NCOL, 256, pxall_i), 0.0)
    c_i[t, c] = (projected(a_i, NCOL, woi) + tokens).astype(BF16)
    send_pooled_img()
    await_z_other()
    i1.s1()
    t1.s3(3, 1)
    recv_txt(CC, c_t)
    t1.s3(2)
    i1.s2()
    t1.s4()
    i1.s2b()
    drain_z()
    drain_small(PX, pxs_i, pxs_t)
    drain_small(AA, a_i, a_t)
    to_partner(1, bs_t, br_t).wait_send()
    recv_pooled_img()
    loss()
    t1.from_sibling()
    fwd_txt(u, False)
    i1.s3(0)
    drain_pooled()
    recv_img(EE, e_i)
    dhidden(e_i, NCOL, woi, fs_i, True)
    f_i[c] = fs_i[c]
    send_img(FF, lambda to: fs_i.at[to], f_i)
    i1.s3(3)
    recv_txt(EE, e_t)
    dhidden(e_t, NROW, wot, fs_t, False)
    f_t[r] = fs_t[r]
    send_txt(FF, lambda to: fs_t.at[to], f_t)
    t1.drain()
    i1.s3(1, 2)
    fwd_img(i1, False, 0, 1)
    recv_img(FF, f_i)
    f2s[0] = hidden_sum(f_i, NCOL, dh_i)
    to_partner(2, f2s.at[0], f2r.at[0]).start()
    i1.s4()
    acc_i[...] = back_img(True, t)
    recv_txt(FF, f_t)
    f2s[1] = hidden_sum(f_t, NROW, dh_t)
    to_partner(3, f2s.at[1], f2r.at[1]).start()
    acc_t[...] = back_txt(t)
    fwd_img(i1, False, 1, 4)
    drain_small(EE, es_i, es_t)
    drain_small(FF, fs_i, fs_t)
    i1.drain()
    to_partner(2, f2s.at[0], f2r.at[0]).wait_recv()
    hidden_other(f2r[0], dh_i)
    finish_img()
    to_partner(3, f2s.at[1], f2r.at[1]).wait_recv()
    hidden_other(f2r[1], dh_t)
    finish_txt()

    to_partner(2, f2s.at[0], f2r.at[0]).wait_send()
    to_partner(3, f2s.at[1], f2r.at[1]).wait_send()


def vm(*shape, dtype=F32):
    return pltpu.VMEM(shape, dtype)


SCRATCH = [
    vm(2, NROW, 4, 2, 192, 128, dtype=BF16), vm(4, 2, RHO, HID, dtype=BF16), vm(2, NROW, 2, 48, HID, dtype=BF16),
    vm(MI, D, dtype=BF16), vm(MT, D, dtype=BF16),
    vm(192, HID, dtype=BF16), vm(96, HID, dtype=BF16), vm(256, HID, dtype=BF16), vm(128, HID, dtype=BF16),
    vm(384, 512, dtype=BF16),
    vm(2, 8, MI, 256), vm(2, 4, MT, 512), vm(8, 8, 256), vm(4, 8, 512),
    vm(MI, HALF), vm(MT, HALF), vm(MI, 512, dtype=BF16), vm(MT, 512, dtype=BF16),
    vm(MI, 512, dtype=BF16), vm(MT, 512, dtype=BF16),
    vm(NCOL, IPD, 384), vm(NROW, IPD, 128), vm(NCOL, IPD, 384), vm(NROW, IPD, 128), vm(32, 384), vm(64, 128),
    vm(NCOL, 16, 512, dtype=BF16), vm(NROW, 16, 512, dtype=BF16), vm(16, 512), vm(64, HID),
    vm(64, 128), vm(64, 128),
    vm(2, NCOL, 32, 256, dtype=BF16), vm(NROW, 64, 128, dtype=BF16), vm(32, PAD), vm(64, PAD),
    vm(NCOL, 32, 256, dtype=BF16), vm(NROW, 64, 128, dtype=BF16),
    vm(NCOL, 32, 256, dtype=BF16), vm(NROW, 64, 128, dtype=BF16),
    vm(NCOL, 16, 640, dtype=BF16), vm(NROW, 16, 640, dtype=BF16),
    vm(NCOL, 16, 640, dtype=BF16), vm(NROW, 16, 640, dtype=BF16),
    vm(16, 128), vm(2, 16, 512, dtype=BF16), vm(2, 16, 512, dtype=BF16), vm(8, 8, 512), vm(8, 8, 512), vm(16, 1024),
    pltpu.SemaphoreType.DMA((4, 32)), pltpu.SemaphoreType.DMA((4, 32)),
    pltpu.SemaphoreType.DMA((17,)), pltpu.SemaphoreType.DMA((17,)),
    pltpu.SemaphoreType.DMA((12,)), pltpu.SemaphoreType.DMA((NROW,)),
    pltpu.SemaphoreType.DMA((5, 24)), pltpu.SemaphoreType.DMA((5, 24)),
    pltpu.SemaphoreType.DMA((4,)), pltpu.SemaphoreType.DMA((4,)),
    pltpu.SemaphoreType.DMA((NCOL,)), pltpu.SemaphoreType.DMA((NCOL,)),
]


def shards(patches, counts, text, partner, scale, shift, img_w_in, img_w_out, txt_w_in, txt_w_out):
    smem = pl.BlockSpec(memory_space=pltpu.SMEM)
    hbm = pl.BlockSpec(memory_space=pl.ANY)
    grad_i, grad_t = pl.pallas_call(
        kernel,
        out_shape=(pltpu.VMEM((MI, HALF), BF16), pltpu.VMEM((MT, HALF), BF16)),
        in_specs=[smem] * 4 + [hbm] * 6,
        out_specs=(pl.BlockSpec(memory_space=pltpu.VMEM),) * 2,
        scratch_shapes=SCRATCH,
        compiler_params=pltpu.CompilerParams(
            collective_id=0, has_side_effects=True, vmem_limit_bytes=58 * 2**20
        ),
        name="towers",
    )(
        counts, partner, scale, shift, patches.reshape(MI, D), text.reshape(MT, D),
        img_w_in, img_w_out.T, txt_w_in, txt_w_out.T,
    )
    return grad_i.reshape(IPD, SLOTS, HALF), grad_t.reshape(IPD, TOKENS, HALF)


def solution(mesh):
    return jax.shard_map(
        shards,
        mesh=mesh,
        in_specs=(
            P(("row", "col"), None, None), P(("row", "col")), P(("col", "row"), None, None), P(), P(), P(),
            P("col", "tp"), P("tp", "col"), P("row", "tp"), P("tp", "row"),
        ),
        out_specs=(P(("row", "col"), None, "tp"), P(("col", "row"), None, "tp")),
        check_vma=False,
    )
```

```python
import jax
import jax.numpy as jnp
from jax import lax
from jax.experimental import pallas as pl
from jax.experimental.pallas import tpu as pltpu
from jax.sharding import PartitionSpec as P

F32, BF16 = jnp.float32, jnp.bfloat16
TXT, IMG = 0, 1
NROW, NCOL, SIDE = 16, 8, 4
D, HID, HALF, PAD = 1536, 2048, 768, 2048
IPD, SLOTS, TOKENS = 4, 128, 64
MI, MT = IPD * SLOTS, IPD * TOKENS
PX, AA, CC, EE, FF = range(5)
RHO = 96
NT = (((1,), (1,)), ((), ()))


def mm(a, b):
    return jnp.dot(a, b, preferred_element_type=F32)


def mm_nt(a, b):
    return lax.dot_general(a, b, NT, preferred_element_type=F32)


def split(v):
    hi = v.astype(BF16)
    return hi, (v - hi.astype(F32)).astype(BF16)


def kernel(
    counts, partner, scale, shift, xi_h, xt_h, wii_h, woi_h, wit_h, wot_h,
    out_i, out_t,
    wi, wz, wt, xi, xt, woi_raw, wot_raw, woi, wot, sel,
    sp_i, sp_t, hp_i, hp_t, acc_i, acc_t, dpre_i, dpre_t, dpre_i2, dpre_t2,
    px_i, px_t, pxs_i, pxs_t, pxall_i, pxall_t, a_i, a_t, stage, ph,
    bs_t, br_t, c_i, c_t, pool_i, pool_t,
    es_i, es_t, e_i, e_t, fs_i, fs_t, f_i, f_t, tail, f2s, f2r, dh_i, dh_t, dtp,
    gs, gr, zs, zr, ls, os_, ms, mr, bs, br, xs, xr,
):
    r, c, t = lax.axis_index("row"), lax.axis_index("col"), lax.axis_index("tp")
    x, y = lax.div(r, SIDE), lax.rem(r, SIDE)
    zlo, k = lax.div(c, 2), lax.rem(c, 2)
    u = 1 - t
    pf = x * (1 - k) + y * k
    qf = y * (1 - k) + x * k
    am, bm = 4 - 3 * k, 1 + 3 * k

    def row_of(f, q):
        return f * am + q * bm

    def turn(v, by):
        return lax.rem(v + by, SIDE)

    def remote(src, dst, ssem, rsem, dev):
        return pltpu.make_async_remote_copy(
            src_ref=src, dst_ref=dst, send_sem=ssem, recv_sem=rsem,
            device_id=dev, device_id_type=pl.DeviceIdType.MESH,
        )

    own_cols = pl.ds(pl.multiple_of(128 * r, 128), 128)
    own_rows = pl.ds(pl.multiple_of(48 * k, 16), 48)

    whole_rows, block_rows = pl.ds(192 - RHO, RHO), pl.ds(0, 192 - RHO)

    def own_block(i):
        cols = pl.ds(pl.multiple_of(128 * i, 128), 128)
        return pltpu.make_async_copy(wii_h.at[block_rows, cols], wi.at[t, i, 0, k, block_rows], os_.at[i])

    locals_ = [
        pltpu.make_async_copy(wit_h.at[own_rows], wt.at[t, r, k], ls.at[0]),
        pltpu.make_async_copy(wii_h.at[whole_rows], wz.at[0, k], ls.at[1]),
        pltpu.make_async_copy(xt_h, xt, ls.at[3]),
        pltpu.make_async_copy(woi_h, woi_raw, ls.at[4]),
        pltpu.make_async_copy(wot_h, wot_raw, ls.at[5]),
    ]
    for i in range(SIDE):
        span = pl.ds(pl.multiple_of(384 * turn(zlo, i), 128), 384)
        locals_.append(pltpu.make_async_copy(xi_h.at[:, span], xi.at[:, 384 * i:384 * (i + 1)], ls.at[8 + i]))
    for copy in locals_:
        copy.start()

    @pl.loop(0, NROW)
    def _(i):
        own_block(i).start()

    barrier = pltpu.get_barrier_semaphore()

    def greet(dev):
        pl.semaphore_signal(barrier, inc=1, device_id=dev, device_id_type=pl.DeviceIdType.MESH)

    @pl.loop(1, NCOL)
    def _(i):
        greet({"col": lax.rem(c + i, NCOL)})

    @pl.loop(1, NROW)
    def _(i):
        greet({"row": lax.rem(r + i, NROW)})

    @pl.loop(0, NCOL)
    def _(i):
        greet({"col": lax.rem(c + i, NCOL), "tp": u})

    pl.semaphore_wait(barrier, 7 + 15 + 8)

    def z_img_same(i, slot):
        return remote(
            wii_h.at[block_rows, own_cols], wi.at[t, r, slot, k, block_rows], zs.at[i], zr.at[i],
            {"col": 2 * turn(zlo, i) + k},
        )

    def z_img_whole(i, slot):
        return remote(
            wii_h.at[whole_rows], wz.at[slot, k], zs.at[8 + i], zr.at[8 + i], {"col": 2 * turn(zlo, i) + k}
        )

    def z_img_other(i, half, slot):
        return remote(
            wii_h.at[:, own_cols], wi.at[half, r, slot, k], zs.at[4 + i], zr.at[4 + i],
            {"col": 2 * turn(zlo, i) + k, "tp": u},
        )

    def z_txt(half, to, sem):
        return remote(wit_h.at[own_rows], wt.at[half, r, k], zs.at[sem], zr.at[8], {"col": 2 * to + k, "tp": u})

    def z_txt_each(act):
        @pl.when(zlo == 3)
        def _():
            act(z_txt(t, 0, 8))
            act(z_txt(t, 1, 0))

        @pl.when(zlo == 0)
        def _():
            act(z_txt(t, 3, 8))
            act(z_txt(t, 2, 0))

    sibling = {"col": c + 1 - 2 * k}

    def whole_to_sibling(i, core):
        ref = wz.at[i, core]
        return remote(ref, ref, zs.at[12 + i], zr.at[12 + i], sibling)

    def own_to_sibling(core):
        ref = wi.at[t, :, 0, core, block_rows]
        return remote(ref, ref, zs.at[16], zr.at[16], sibling)

    @pl.loop(1, SIDE)
    def _(i):
        z_img_same(i, SIDE - i).start()

    def z_later():
        @pl.loop(0, SIDE)
        def _(i):
            z_img_other(i, t, lax.rem(SIDE - i, SIDE)).start()

    dev_p = [{"row": row_of(turn(pf, 1), qf)}, {"row": row_of(turn(pf, 3), qf)}]
    dev_q = [{"row": row_of(pf, turn(qf, 1))}, {"row": row_of(pf, turn(qf, 3))}]
    class Batch:
        def __init__(self, n, tower, half):
            self.n, self.tower, self.half = n, tower, half
            own = n == 1
            self.first, self.rows = (1, 192 - RHO) if own else (0, 192)

        def shard(self, row, core=None):
            core = k if core is None else core
            if self.tower == TXT:
                return wt.at[self.half, row, core]
            return self.block(row, core, 0, self.rows)

        def block(self, row, core, start, rows):
            return wi.at[self.half, row, self.first:SIDE, core, pl.ds(start, rows)]

        def part(self, row, h):
            if self.tower == TXT:
                return wt.at[self.half, row, k, :, pl.ds(1024 * h, 1024)]
            return self.block(row, k, self.rows // 2 * h, self.rows // 2)

        def copy(self, index, ref, dev):
            return remote(ref, ref, gs.at[self.n, index], gr.at[self.n, index], dev)

        def to_sibling(self, row):
            self.copy(16 + row, self.shard(row), sibling).start()

        def spread(self, j):
            row = row_of(turn(pf, j), qf)
            ref = self.shard(row)
            self.copy(4 + 2 * j, ref, dev_q[0]).start()
            self.copy(5 + 2 * j, ref, dev_q[1]).start()
            self.to_sibling(row)

        def s1(self):
            ref = self.shard(r)
            self.copy(0, ref, dev_p[0]).start()
            self.copy(1, ref, dev_p[1]).start()
            self.spread(0)

        def s2(self):
            left, right = row_of(turn(pf, 3), qf), row_of(turn(pf, 1), qf)
            self.copy(0, self.shard(left), dev_p[0]).wait_recv()
            self.copy(2, self.part(left, 0), dev_p[0]).start()
            self.copy(1, self.shard(right), dev_p[1]).wait_recv()
            self.copy(3, self.part(right, 1), dev_p[1]).start()
            self.spread(3)
            self.spread(1)

        def s2b(self):
            far = row_of(turn(pf, 2), qf)
            self.copy(2, self.part(far, 0), dev_p[0]).wait_recv()
            self.copy(3, self.part(far, 1), dev_p[1]).wait_recv()
            self.spread(2)

        def s3(self, *js):
            for j in js:
                for way, at in ((0, 3), (1, 1)):
                    row = row_of(turn(pf, j), turn(qf, at))
                    ref = self.shard(row)
                    self.copy(4 + 2 * j + way, ref, dev_q[way]).wait_recv()
                    if (j in (0, 1)) == (way == 0):
                        self.copy(12 + j, ref, dev_q[way]).start()
                    self.to_sibling(row)

        def s4(self):
            for j in (0, 3, 1, 2):
                row = row_of(turn(pf, j), turn(qf, 2))
                self.copy(12 + j, self.shard(row), dev_q[0]).wait_recv()
                self.to_sibling(row)

        def from_sibling(self):
            @pl.loop(0, NROW)
            def _(row):
                self.row_from_sibling(row)

        def row_from_sibling(self, row):
            self.copy(16 + row, self.shard(row, 1 - k), sibling).wait_recv()

        def drain(self):
            for j in (0, 1):
                self.copy(j, self.shard(r), dev_p[j]).wait_send()
                self.copy(2 + j, self.part(r, j), dev_p[j]).wait_send()

            @pl.loop(4, 32)
            def _(i):
                self.copy(i, self.shard(r), dev_q[0]).wait_send()

    t0, i0, t1, i1 = Batch(0, TXT, t), Batch(1, IMG, t), Batch(2, TXT, u), Batch(3, IMG, u)

    def send_img(stage_id, src, dst):
        @pl.loop(1, NCOL)
        def _(i):
            to = lax.rem(c + i, NCOL)
            remote(src(to), dst.at[c], ms.at[stage_id, i], mr.at[stage_id, i], {"col": to}).start()

    def send_txt(stage_id, src, dst):
        @pl.loop(1, NROW)
        def _(i):
            to = lax.rem(r + i, NROW)
            remote(src(to), dst.at[r], ms.at[stage_id, 8 + i], mr.at[stage_id, 8 + i], {"row": to}).start()

    def recv_img(stage_id, dst):
        @pl.loop(1, NCOL)
        def _(i):
            ref = dst.at[lax.rem(c + NCOL - i, NCOL)]
            remote(ref, ref, ms.at[stage_id, i], mr.at[stage_id, i], {"col": lax.rem(c + i, NCOL)}).wait_recv()

    def recv_txt(stage_id, dst):
        @pl.loop(1, NROW)
        def _(i):
            ref = dst.at[lax.rem(r + NROW - i, NROW)]
            remote(ref, ref, ms.at[stage_id, 8 + i], mr.at[stage_id, 8 + i], {"row": lax.rem(r + i, NROW)}).wait_recv()

    def drain_small(stage_id, src_i, src_t):
        @pl.loop(1, NCOL)
        def _(i):
            remote(src_i.at[c], src_i.at[c], ms.at[stage_id, i], mr.at[stage_id, i], {"col": lax.rem(c + i, NCOL)}).wait_send()

        @pl.loop(1, NROW)
        def _(i):
            remote(
                src_t.at[r], src_t.at[r], ms.at[stage_id, 8 + i], mr.at[stage_id, 8 + i], {"row": lax.rem(r + i, NROW)}
            ).wait_send()

    def live(i, width):
        return lax.broadcasted_iota(jnp.int32, (SLOTS, width), 0) < counts[i]

    def counted(i, width):
        return jnp.full((1, width), counts[i], jnp.int32).astype(F32)

    def local_part():
        d = lax.broadcasted_iota(jnp.int32, (384, 512), 0)
        e = lax.broadcasted_iota(jnp.int32, (384, 512), 1)
        hit = ((e & 127) < 96) & (d == (e >> 7) * 96 + (e & 127))
        sel[...] = jnp.where(hit, 1.0, 0.0).astype(BF16)
        for copy in locals_[2:]:
            copy.wait()
        row = lax.broadcasted_iota(jnp.int32, (8, MI), 0)
        tok = lax.broadcasted_iota(jnp.int32, (8, MI), 1)
        limit = jnp.zeros((8, MI), jnp.int32)
        for i in range(IPD):
            limit = jnp.where(row == i, counts[i], limit)
        mask_i = jnp.where((tok >= SLOTS * row) & (tok < SLOTS * row + limit), 1.0, 0.0).astype(BF16)
        row = lax.broadcasted_iota(jnp.int32, (8, MT), 0)
        tok = lax.broadcasted_iota(jnp.int32, (8, MT), 1)
        mask_t = jnp.where((tok >= TOKENS * row) & (tok < TOKENS * row + TOKENS), 1.0, 0.0).astype(BF16)
        sub = lax.broadcasted_iota(jnp.int32, (8, 128), 0)
        cnt = jnp.full((8, 128), 1, jnp.int32)
        for i in range(IPD):
            cnt = jnp.where(sub == i, counts[i], cnt)
        cnt = cnt.astype(F32)
        for p in range(NCOL):
            pxs_i[p, :, 256:] = cnt[0:IPD]
        sums_i = mm(mask_i, xi[...]) / cnt[:, 0:1]
        sums_t = mm(mask_t, xt[...]) / float(TOKENS)
        for sums, dst, per in ((sums_i, pxs_i, 256), (sums_t, pxs_t, 128)):
            hi, lo = split(sums)
            both = jnp.concatenate([hi.astype(F32), lo.astype(F32)], axis=0).astype(BF16)
            for g in range(4):
                wide = mm(both[:, 384 * g:384 * (g + 1)], sel[...])
                wide = (wide[0:8] + wide[8:16])[0:IPD]
                first = 2 * turn(zlo, g) if per == 256 else 4 * g
                for p in range(512 // per):
                    dst[first + p, :, 0:per] = wide[:, per * p:per * (p + 1)]
        px_i[c] = pxs_i[c]
        px_t[r] = pxs_t[r]
        send_img(PX, lambda to: pxs_i.at[to], px_i)
        send_txt(PX, lambda to: pxs_t.at[to], px_t)

    def pooled_tokens(src, peers, width, dst):
        for p in range(peers):
            dst[4 * p:4 * p + 4, :] = src[p]
        return dst[:, 0:width]

    def pad_out():
        for raw, dst, narrow, wide in ((woi_raw, woi, 192, 256), (wot_raw, wot, 96, 128)):
            e = lax.broadcasted_iota(jnp.int32, (wide, narrow), 0)
            d = lax.broadcasted_iota(jnp.int32, (wide, narrow), 1)
            hit = ((e & 127) < 96) & (d == (e >> 7) * 96 + (e & 127))
            dst[...] = mm(jnp.where(hit, 1.0, 0.0).astype(BF16), raw[...]).astype(BF16)

    def img_rows(own, half, row, ds):
        if not own:
            return jnp.concatenate([wi[half, row, d].reshape(384, 128) for d in ds], axis=0)
        cols = pl.ds(pl.multiple_of(128 * row, 128), 128)
        return jnp.concatenate(
            [v for d in ds for h in (0, 1) for v in (wi[half, row, d, h, block_rows], wz[d, h, :, cols])], axis=0
        )

    def img_block(own, half, p, pooled):
        w = jnp.concatenate([img_rows(own, half, 2 * p + j, range(SIDE)) for j in (0, 1)], axis=1)
        pre = mm(xi[...], w)
        for i in range(IPD):
            v = 0.5 * pre[SLOTS * i:SLOTS * (i + 1)]
            th = jnp.tanh(v)
            on = live(i, 256)
            slope = 0.5 * (1.0 + th) * (1.0 + v * (1.0 - th))
            sp_i[half, p, SLOTS * i:SLOTS * (i + 1), :] = jnp.where(on, slope, 0.0)
            if pooled:
                total = jnp.sum(jnp.where(on, v + v * th, 0.0), axis=0, keepdims=True)
                hp_i[p, i:i + 1, :] = total / counted(i, 256)

    def fwd_img(batch, pooled, first, last):
        near = lax.div(y, 2)

        def block_of(n):
            m, e = lax.rem(n, 4), lax.div(n, 4)
            along = m + lax.div(m, 2) * (1 - 2 * lax.rem(m, 2))
            return 2 * turn(x, along) + near + e * (1 - 2 * near)

        @pl.loop(first, last)
        def _(n):
            ps = [block_of(2 * n), block_of(2 * n + 1)]
            for p in ps:
                batch.row_from_sibling(2 * p)
                batch.row_from_sibling(2 * p + 1)
            for p in ps:
                img_block(batch.n == 1, batch.half, p, pooled)

    def fwd_txt(half, pooled):
        @pl.loop(0, 4, unroll=2)
        def _(n):
            w = wt[half, :, :, :, pl.ds(pl.multiple_of(512 * n, 512), 512)].reshape(D, 512)
            pre = mm(xt[...], w)
            for i in range(IPD):
                v = 0.5 * pre[TOKENS * i:TOKENS * (i + 1)]
                th = jnp.tanh(v)
                sp_t[half, n, TOKENS * i:TOKENS * (i + 1), :] = 0.5 * (1.0 + th) * (1.0 + v * (1.0 - th))
                if pooled:
                    hp_t[n, i:i + 1, :] = jnp.sum(v + v * th, axis=0, keepdims=True) / float(TOKENS)

    def send_hidden_img():
        for q in range(4):
            for h in range(2):
                stage[4 * q:4 * q + 4, 256 * h:256 * (h + 1)] = hp_i[2 * q + h, 0:IPD]
        a_i[c] = stage[...].astype(BF16)
        send_img(AA, lambda to: a_i.at[c], a_i)

    def send_hidden_txt():
        for q in range(4):
            stage[4 * q:4 * q + 4, :] = hp_t[q, 0:IPD]
        a_t[r] = stage[...].astype(BF16)
        send_txt(AA, lambda to: a_t.at[r], a_t)

    def projected(src, peers, w):
        for p in range(peers):
            block = src[p].astype(F32)
            for q in range(4):
                ph[4 * p:4 * p + 4, 512 * q:512 * (q + 1)] = block[4 * q:4 * q + 4]
        return mm_nt(ph[0:4 * peers].astype(BF16), w[...])

    def to_partner(index, src, dst):
        return remote(src, dst, bs.at[index], br.at[index], {"tp": u})

    def to_other(i, half, slot):
        ref = c_i.at[half, slot]
        return remote(ref, ref, xs.at[i], xr.at[i], {"col": lax.rem(c + i, NCOL), "tp": u})

    def send_pooled_img():
        @pl.loop(0, NCOL)
        def _(i):
            to_other(i, t, c).start()

        send_img(CC, lambda to: c_i.at[t, c], c_i.at[t])

    def recv_pooled_img():
        @pl.loop(0, NCOL)
        def _(i):
            to_other(i, u, lax.rem(c + NCOL - i, NCOL)).wait_recv()

        recv_img(CC, c_i.at[t])

    def norm_of(pool):
        inv = lax.rsqrt(jnp.sum(pool * pool, axis=-1, keepdims=True) + 1e-6)
        return pool * inv, inv

    def loss():
        for p in range(NCOL):
            pool_i[:, 256 * p:256 * (p + 1)] = c_i[0, p].astype(F32) + c_i[1, p].astype(F32)
        for p in range(NROW):
            pool_t[:, 128 * p:128 * (p + 1)] = c_t[p].astype(F32)
        emb_i, inv_i = norm_of(pool_i[...])
        emb_t, inv_t = norm_of(pool_t[...])
        ih, il = split(emb_i)
        th, tl = split(emb_t)
        ni, nt = 32, 64
        one = mm_nt(jnp.concatenate([ih, il], axis=0), th)
        cos = one[0:ni] + one[ni:] + mm_nt(ih, tl)
        two = mm_nt(jnp.concatenate([th, tl], axis=0), ih)
        cos_t = two[0:nt] + two[nt:] + mm_nt(th, il)
        temp, bias = scale[0], shift[0]
        row = lax.broadcasted_iota(jnp.int32, (ni, nt), 0)
        lane = lax.broadcasted_iota(jnp.int32, (nt, ni), 1)
        mate = jnp.zeros((ni, nt), jnp.int32)
        mate_t = jnp.zeros((nt, ni), jnp.int32)
        for i in range(ni):
            text = partner[r * ni + i]
            mate = jnp.where(row == i, text, mate)
            mate_t = jnp.where(lane == i, text, mate_t)

        def slopes(value, other, ids):
            sign = jnp.where(other == ids, 1.0, -1.0)
            return -sign * jax.nn.sigmoid(-sign * (temp * value + bias))

        dl = slopes(cos, mate, c * nt + lax.broadcasted_iota(jnp.int32, (ni, nt), 1))
        dl_t = slopes(cos_t, mate_t, c * nt + lax.broadcasted_iota(jnp.int32, (nt, ni), 0))
        dh, dlo = split(dl)
        one = mm(jnp.concatenate([dh, dlo], axis=0), th)
        g_i = one[0:ni] + one[ni:] + mm(dh, tl)
        dh, dlo = split(dl_t)
        two = mm(jnp.concatenate([dh, dlo], axis=0), ih)
        g_t = two[0:nt] + two[nt:] + mm(dh, il)
        q_i = jnp.sum(dl * cos, axis=-1, keepdims=True)
        q_t = jnp.sum(dl_t * cos_t, axis=-1, keepdims=True)
        part_i = (g_i - emb_i * q_i) * (temp * inv_i / pxall_i[:, 256:257])
        part_t = (g_t - emb_t * q_t) * (temp * inv_t * (1.0 / TOKENS))
        for p in range(NCOL):
            es_i[p] = part_i[:, 256 * p:256 * (p + 1)].astype(BF16)
        for p in range(NROW):
            es_t[p] = part_t[:, 128 * p:128 * (p + 1)].astype(BF16)
        e_i[c] = es_i[c]
        e_t[r] = es_t[r]
        send_txt(EE, lambda to: es_t.at[to], e_t)
        send_img(EE, lambda to: es_i.at[to], e_i)

    def dhidden(src, peers, w, dst, wide):
        total = src[0].astype(F32)
        for p in range(1, peers):
            total = total + src[p].astype(F32)
        hi, lo = split(total)
        hidden = mm(hi, w[...])
        hi, lo = hi.astype(F32), lo.astype(F32)
        for p in range(peers):
            rows = slice(4 * p, 4 * p + 4)
            for q in range(4):
                stage[4 * q:4 * q + 4, :] = hidden[rows, 512 * q:512 * (q + 1)]
            dst[p, :, 0:512] = stage[...].astype(BF16)
            tail[0:4, :] = hi[rows, 0:128]
            tail[8:12, :] = lo[rows, 0:128]
            if wide:
                tail[4:8, :] = hi[rows, 128:256]
                tail[12:16, :] = lo[rows, 128:256]
            dst[p, :, 512:640] = tail[...].astype(BF16)

    def hidden_sum(src, peers, dst):
        total = src[0, :, 0:512].astype(F32)
        for p in range(1, peers):
            total = total + src[p, :, 0:512].astype(F32)
        stage[...] = total
        for q in range(4):
            dst[4 * t + q, 0:IPD, :] = stage[4 * q:4 * q + 4, :]
        return total.astype(BF16)

    def hidden_other(src, dst):
        stage[...] = src.astype(F32)
        for q in range(4):
            dst[4 * u + q, 0:IPD, :] = stage[4 * q:4 * q + 4, :]

    def back(piece, add, bufs):
        piece(0, bufs[0])
        piece(1, bufs[1])
        total = add(0, bufs[0])
        piece(2, bufs[0])
        total += add(1, bufs[1])
        piece(3, bufs[1])
        total += add(2, bufs[0])
        return total + add(3, bufs[1])

    def back_img(own, half):
        def piece(n, dst):
            for h in range(2):
                for i in range(IPD):
                    at = slice(SLOTS * i, SLOTS * (i + 1))
                    slope = sp_i[half, 2 * n + h, at, :]
                    dst[at, 256 * h:256 * (h + 1)] = (
                        slope * dh_i[4 * half + n, i:i + 1, 256 * h:256 * (h + 1)]
                    ).astype(BF16)

        def add(n, src):
            ds = [lax.rem(2 * t + j + SIDE - zlo, SIDE) for j in (0, 1)]
            w = jnp.concatenate([img_rows(own, half, 4 * n + j, ds) for j in range(4)], axis=1)
            return mm_nt(src[...], w)

        return back(piece, add, (dpre_i, dpre_i2))

    def back_txt(half):
        def piece(n, dst):
            for i in range(IPD):
                at = slice(TOKENS * i, TOKENS * (i + 1))
                dst[at, :] = (sp_t[half, n, at, :] * dh_t[4 * half + n, i:i + 1, :]).astype(BF16)

        def add(n, src):
            w = wt[half, pl.ds(8 * t, 8), :, :, pl.ds(512 * n, 512)].reshape(HALF, 512)
            return mm_nt(src[...], w)

        return back(piece, add, (dpre_t, dpre_t2))

    def token_part(src, wide):
        if wide:
            for p in range(4):
                block = src[4 * t + p, :, 512:640].astype(F32)
                for h in range(2):
                    at = slice(256 * p + 128 * h, 256 * p + 128 * (h + 1))
                    dtp[0:4, at] = block[4 * h:4 * h + 4]
                    dtp[8:12, at] = block[8 + 4 * h:12 + 4 * h]
        else:
            for p in range(8):
                dtp[:, 128 * p:128 * (p + 1)] = src[8 * t + p, :, 512:640].astype(F32)
        natural = [mm_nt(dtp[:, 512 * g:512 * (g + 1)].astype(BF16), sel[...]) for g in range(2)]
        natural = jnp.concatenate(natural, axis=1)
        return natural[0:8] + natural[8:16]

    def finish_txt():
        token = token_part(f_t, False)
        acc_t[...] += back_txt(u)
        for i in range(IPD):
            at = slice(TOKENS * i, TOKENS * (i + 1))
            out_t[at, :] = (acc_t[at, :] + token[i:i + 1]).astype(BF16)

    def finish_img():
        token = token_part(f_i, True)
        acc_i[...] += back_img(False, u)
        for i in range(IPD):
            at = slice(SLOTS * i, SLOTS * (i + 1))
            out_i[at, :] = (acc_i[at, :] + jnp.where(live(i, HALF), token[i:i + 1], 0.0)).astype(BF16)

    def await_z_same():
        @pl.loop(1, SIDE)
        def _(i):
            z_img_same(i, i).wait_recv()

    def await_z_whole():
        locals_[1].wait()
        whole_to_sibling(0, k).start()

        @pl.loop(1, SIDE)
        def _(i):
            z_img_whole(i, SIDE - i).wait_recv()
            whole_to_sibling(SIDE - i, k).start()

    def await_sibling_whole():
        own_to_sibling(1 - k).wait_recv()

        @pl.loop(0, SIDE)
        def _(i):
            whole_to_sibling(i, 1 - k).wait_recv()

    def await_z_other():
        @pl.loop(0, SIDE)
        def _(i):
            z_img_other(i, u, i).wait_recv()

    def drain_z():
        @pl.loop(1, SIDE)
        def _(i):
            z_img_same(i, SIDE - i).wait_send()
            z_img_whole(i, SIDE - i).wait_send()

        @pl.loop(0, SIDE)
        def _(i):
            whole_to_sibling(i, k).wait_send()
            z_img_other(i, t, lax.rem(SIDE - i, SIDE)).wait_send()

        z_txt_each(lambda copy: copy.wait_send())
        own_to_sibling(k).wait_send()

    def drain_pooled():
        @pl.loop(0, NCOL)
        def _(i):
            to_other(i, t, c).wait_send()

        drain_small(CC, c_i.at[t], c_t)

    locals_[0].wait()
    t0.s1()
    z_txt_each(lambda copy: copy.start())

    @pl.loop(1, SIDE)
    def _(i):
        z_img_whole(i, SIDE - i).start()

    t0.s2()
    t0.s2b()
    await_z_same()
    i0.s1()

    @pl.loop(0, NROW)
    def _(i):
        own_block(i).wait()

    own_to_sibling(k).start()
    tail[...] = jnp.zeros_like(tail)
    dtp[...] = jnp.zeros_like(dtp)
    t0.s3(0)
    i0.s2()
    local_part()
    z_later()
    t0.s3(3, 1)
    i0.s2b()
    t0.s3(2)
    pad_out()
    t0.s4()
    i0.s3(0, 3)
    t0.from_sibling()
    fwd_txt(t, True)
    send_hidden_txt()
    await_z_whole()
    z_txt(u, zlo, 8).wait_recv()
    t1.s1()
    i0.s3(1, 2)
    recv_txt(AA, a_t)
    bs_t[...] = projected(a_t, NROW, wot)
    to_partner(1, bs_t, br_t).start()
    await_sibling_whole()
    fwd_img(i0, True, 0, 1)
    i0.s4()
    fwd_img(i0, True, 1, 2)
    t1.s2()
    to_partner(1, bs_t, br_t).wait_recv()
    recv_txt(PX, px_t)
    c_t[r] = (bs_t[...] + br_t[...] + pooled_tokens(px_t, NROW, 128, pxall_t)).astype(BF16)
    send_txt(CC, lambda to: c_t.at[r], c_t)
    fwd_img(i0, True, 2, 4)
    send_hidden_img()
    t1.s2b()
    t1.s3(0)
    t0.drain()
    i0.drain()
    recv_img(AA, a_i)
    recv_img(PX, px_i)
    tokens = jnp.where(t == 0, pooled_tokens(px_i, NCOL, 256, pxall_i), 0.0)
    c_i[t, c] = (projected(a_i, NCOL, woi) + tokens).astype(BF16)
    send_pooled_img()
    await_z_other()
    i1.s1()
    t1.s3(3, 1)
    recv_txt(CC, c_t)
    t1.s3(2)
    i1.s2()
    t1.s4()
    i1.s2b()
    drain_z()
    drain_small(PX, pxs_i, pxs_t)
    drain_small(AA, a_i, a_t)
    to_partner(1, bs_t, br_t).wait_send()
    recv_pooled_img()
    loss()
    t1.from_sibling()
    fwd_txt(u, False)
    i1.s3(0)
    drain_pooled()
    recv_img(EE, e_i)
    dhidden(e_i, NCOL, woi, fs_i, True)
    f_i[c] = fs_i[c]
    send_img(FF, lambda to: fs_i.at[to], f_i)
    i1.s3(3)
    recv_txt(EE, e_t)
    dhidden(e_t, NROW, wot, fs_t, False)
    f_t[r] = fs_t[r]
    send_txt(FF, lambda to: fs_t.at[to], f_t)
    t1.drain()
    i1.s3(1, 2)
    fwd_img(i1, False, 0, 1)
    recv_img(FF, f_i)
    f2s[0] = hidden_sum(f_i, NCOL, dh_i)
    to_partner(2, f2s.at[0], f2r.at[0]).start()
    i1.s4()
    acc_i[...] = back_img(True, t)
    recv_txt(FF, f_t)
    f2s[1] = hidden_sum(f_t, NROW, dh_t)
    to_partner(3, f2s.at[1], f2r.at[1]).start()
    acc_t[...] = back_txt(t)
    fwd_img(i1, False, 1, 4)
    drain_small(EE, es_i, es_t)
    drain_small(FF, fs_i, fs_t)
    i1.drain()
    to_partner(2, f2s.at[0], f2r.at[0]).wait_recv()
    hidden_other(f2r[0], dh_i)
    finish_img()
    to_partner(3, f2s.at[1], f2r.at[1]).wait_recv()
    hidden_other(f2r[1], dh_t)
    finish_txt()

    to_partner(2, f2s.at[0], f2r.at[0]).wait_send()
    to_partner(3, f2s.at[1], f2r.at[1]).wait_send()


def vm(*shape, dtype=F32):
    return pltpu.VMEM(shape, dtype)


SCRATCH = [
    vm(2, NROW, 4, 2, 192, 128, dtype=BF16), vm(4, 2, RHO, HID, dtype=BF16), vm(2, NROW, 2, 48, HID, dtype=BF16),
    vm(MI, D, dtype=BF16), vm(MT, D, dtype=BF16),
    vm(192, HID, dtype=BF16), vm(96, HID, dtype=BF16), vm(256, HID, dtype=BF16), vm(128, HID, dtype=BF16),
    vm(384, 512, dtype=BF16),
    vm(2, 8, MI, 256), vm(2, 4, MT, 512), vm(8, 8, 256), vm(4, 8, 512),
    vm(MI, HALF), vm(MT, HALF), vm(MI, 512, dtype=BF16), vm(MT, 512, dtype=BF16),
    vm(MI, 512, dtype=BF16), vm(MT, 512, dtype=BF16),
    vm(NCOL, IPD, 384), vm(NROW, IPD, 128), vm(NCOL, IPD, 384), vm(NROW, IPD, 128), vm(32, 384), vm(64, 128),
    vm(NCOL, 16, 512, dtype=BF16), vm(NROW, 16, 512, dtype=BF16), vm(16, 512), vm(64, HID),
    vm(64, 128), vm(64, 128),
    vm(2, NCOL, 32, 256, dtype=BF16), vm(NROW, 64, 128, dtype=BF16), vm(32, PAD), vm(64, PAD),
    vm(NCOL, 32, 256, dtype=BF16), vm(NROW, 64, 128, dtype=BF16),
    vm(NCOL, 32, 256, dtype=BF16), vm(NROW, 64, 128, dtype=BF16),
    vm(NCOL, 16, 640, dtype=BF16), vm(NROW, 16, 640, dtype=BF16),
    vm(NCOL, 16, 640, dtype=BF16), vm(NROW, 16, 640, dtype=BF16),
    vm(16, 128), vm(2, 16, 512, dtype=BF16), vm(2, 16, 512, dtype=BF16), vm(8, 8, 512), vm(8, 8, 512), vm(16, 1024),
    pltpu.SemaphoreType.DMA((4, 32)), pltpu.SemaphoreType.DMA((4, 32)),
    pltpu.SemaphoreType.DMA((17,)), pltpu.SemaphoreType.DMA((17,)),
    pltpu.SemaphoreType.DMA((12,)), pltpu.SemaphoreType.DMA((NROW,)),
    pltpu.SemaphoreType.DMA((5, 24)), pltpu.SemaphoreType.DMA((5, 24)),
    pltpu.SemaphoreType.DMA((4,)), pltpu.SemaphoreType.DMA((4,)),
    pltpu.SemaphoreType.DMA((NCOL,)), pltpu.SemaphoreType.DMA((NCOL,)),
]


def shards(patches, counts, text, partner, scale, shift, img_w_in, img_w_out, txt_w_in, txt_w_out):
    smem = pl.BlockSpec(memory_space=pltpu.SMEM)
    hbm = pl.BlockSpec(memory_space=pl.ANY)
    grad_i, grad_t = pl.pallas_call(
        kernel,
        out_shape=(pltpu.VMEM((MI, HALF), BF16), pltpu.VMEM((MT, HALF), BF16)),
        in_specs=[smem] * 4 + [hbm] * 6,
        out_specs=(pl.BlockSpec(memory_space=pltpu.VMEM),) * 2,
        scratch_shapes=SCRATCH,
        compiler_params=pltpu.CompilerParams(
            collective_id=0, has_side_effects=True, vmem_limit_bytes=58 * 2**20
        ),
        name="towers",
    )(
        counts, partner, scale, shift, patches.reshape(MI, D), text.reshape(MT, D),
        img_w_in, img_w_out.T, txt_w_in, txt_w_out.T,
    )
    return grad_i.reshape(IPD, SLOTS, HALF), grad_t.reshape(IPD, TOKENS, HALF)


def solution(mesh):
    return jax.shard_map(
        shards,
        mesh=mesh,
        in_specs=(
            P(("row", "col"), None, None), P(("row", "col")), P(("col", "row"), None, None), P(), P(), P(),
            P("col", "tp"), P("tp", "col"), P("row", "tp"), P("tp", "row"),
        ),
        out_specs=(P(("row", "col"), None, "tp"), P(("col", "row"), None, "tp")),
        check_vma=False,
    )
```
